32 devices in a mesh: groups: 2 (over x), seq: 16 (over z, y, core).
Axes of the slice: x: 2, y: 2, z: 4, core: 2. Of those that a mesh axis runs over, the one named last changes fastest.
Arguments:
- queries: bfloat16 [4096, 8192], P(('groups', 'seq')), parts along dimension 0, may hold values from -4.5 to 4.5
- keyvalue: bfloat16 [4096, 2048], P(('groups', 'seq')), parts along dimension 0, may hold values from -4.5 to 4.5
- doc_ids: int32 [4096], P(('groups', 'seq')), parts along dimension 0, may hold values from 0 to 7, never falling along the last dimension, each value on 1 to 512 neighbouring positions
- owner_tiles: int32 [32, 2], P(('groups', 'seq')), parts along dimension 0, may hold values from 0 to 15, as said below
- tile_counts: int32 [32], P(('groups', 'seq')), parts along dimension 0, may hold values from 0 to 2, as said below
Outputs:
- owned: bfloat16 [8192, 8192], P(('groups', 'seq')), parts along dimension 0
The draws below stay inside these ranges and needn't reach their ends.
There are 2 independent parts, one for each index of `groups`. The reference program is written for one: setup_inputs(seed, part) draws one part's arguments, and reference() takes and returns one part's arrays. A program takes and returns all parts, laid end to end along the dimension named above; each array names one. Nothing has to cross between parts.
Inputs may be any that keep to these rules, and one draw needn't show every extreme that they name: `owner_tiles`: over the slots below each owner's count, every tile 0 to 15 is listed exactly once; the other slots hold 0. Tile t is listed either by its holder, the owner o with o * 128 <= t * 128 < (o + 1) * 128, or by the holder's partner, the owner whose index differs from the holder's by half the number of owners. `tile_counts`: the counts sum to 16; each is 0, 1 or 2, some owner has 2, and an owner has 2 exactly when its partner has 0.
All inputs are finite; a program needn't handle non-finite values.
Results may differ from the reference program's by a relative error of at most 0.0034.
Values may be sent and summed in bfloat16 or wider, within the bound.
No kernel may reach another device: no remote copies, remote signals or barrier semaphores. Data moves between devices by JAX's collectives and lax.ppermute only.
A program may use at most 64 MiB of HBM per device.

```python
import math
import jax
import jax.numpy as jnp
import numpy as np
from jax import lax

QUERY_HEADS = 64
KEY_VALUE_HEADS = 8
HEAD_WIDTH = 128
TILE = 128
DOCUMENT_LIMIT = 512
TOK_DEV = 128
SLAB_TOKENS = 2048
NTILE = 16
CAP = 2
DOCS = 8
N_SEQ = 16


def draw_queries(key, part):
    owner_key = jax.random.fold_in(key, 11)
    value_rows = jax.random.truncated_normal(owner_key, -4.0, 4.0, (SLAB_TOKENS, QUERY_HEADS, HEAD_WIDTH))
    return value_rows.astype(jnp.float32).reshape(SLAB_TOKENS, QUERY_HEADS * HEAD_WIDTH).astype(jnp.bfloat16)


def draw_keyvalue(key, part):
    owner_key = jax.random.fold_in(key, 23)
    value_rows = jax.random.truncated_normal(owner_key, -4.0, 4.0, (SLAB_TOKENS, KEY_VALUE_HEADS, 2, HEAD_WIDTH))
    return value_rows.astype(jnp.float32).reshape(SLAB_TOKENS, KEY_VALUE_HEADS * 2 * HEAD_WIDTH).astype(jnp.bfloat16)


def owner_plan(key):
    base = jax.random.fold_in(key, 5113)
    leading_entry, second, third, fourth = jax.random.split(base, 4)
    half = N_SEQ // 2
    per_device = TOK_DEV // TILE
    pair_rank = jnp.argsort(jax.random.permutation(leading_entry, half))
    movers = jax.random.randint(second, (), 1, half // 2 + 1)
    moving = pair_rank < movers
    side = jax.random.randint(third, (half,), 0, 2)
    devices = jnp.arange(N_SEQ, dtype=jnp.int32)
    pair = devices % half
    lower = devices < half
    moving_dev = moving[pair]
    giver = moving_dev & ((side[pair] == 0) == lower)
    taker = moving_dev & jnp.logical_not(giver)
    counts = jnp.where(giver, 0, jnp.where(taker, CAP, per_device)).astype(jnp.int32)
    local_tiles = jnp.arange(per_device, dtype=jnp.int32)
    own = devices[:, None] * per_device + local_tiles[None, :]
    partner = (devices + half) % N_SEQ
    theirs = partner[:, None] * per_device + local_tiles[None, :]
    candidates = jnp.concatenate([own, jnp.where(taker[:, None], theirs, 0)], axis=1)
    candidates = jnp.where(giver[:, None], 0, candidates)
    slots = jnp.arange(CAP, dtype=jnp.int32)
    shuffled = jax.random.permutation(fourth, jnp.tile(slots[None, :], (N_SEQ, 1)), axis=1, independent=True)
    scores = shuffled + jnp.where(slots[None, :] < counts[:, None], 0, CAP)
    order = jnp.argsort(scores, axis=1, stable=True)
    lists = jnp.take_along_axis(candidates, order, axis=1)
    lists = jnp.where(slots[None, :] < counts[:, None], lists, 0).astype(jnp.int32)
    return (lists, counts)


def draw_owner_tiles(key, part):
    lists, counts = owner_plan(key)
    return lists


def draw_tile_counts(key, part):
    lists, counts = owner_plan(key)
    return counts


def length_profile(count, total, most, lean):
    portions = [(1 << 20) // math.isqrt(standing ** lean) + 1 for standing in range(2, count + 1)]
    surplus, given = total - most - (count - 1), [1] * (count - 1)
    while surplus > 0:
        free = [i for i in range(count - 1) if given[i] < most]
        whole, left = sum([portions[i] for i in free]), surplus
        for i in free:
            addition = min(most - given[i], max(1, left * portions[i] // whole), surplus)
            given[i] = given[i] + addition
            surplus = surplus - addition
    return np.array([most] + given)


def ragged_sizes(key, number_of, total, most, slope):
    if number_of == 2:
        one = jax.random.randint(key, (), max(1, total - most), min(most, total - 1) + 1)
        return jnp.stack([one, total - one])
    lengths = jnp.asarray(length_profile(number_of, total, most, slope), jnp.int32)
    twos = (number_of - 1) // 2
    donor, taker = lengths[1:1 + 2 * twos:2], lengths[2:2 + 2 * twos:2]
    margin = jnp.minimum(donor - 1, most - taker)
    shifted = jax.random.randint(jax.random.fold_in(key, 1), (twos,), 0, 1 << 20) % (margin + 1)
    lengths = lengths.at[1:1 + 2 * twos:2].set(donor - shifted).at[2:2 + 2 * twos:2].set(taker + shifted)
    return lengths[jax.random.permutation(jax.random.fold_in(key, 2), number_of)]


def setup_inputs(seed: int = 0, part: int = 0) -> dict:
    arg_keys = jax.random.split(jax.random.key(seed), 6)
    part_splits = jax.random.split(jax.random.fold_in(arg_keys[5], part), 6)
    return {
        "queries": draw_queries(jax.random.fold_in(jax.random.fold_in(arg_keys[5], part), 71), part),
        "keyvalue": draw_keyvalue(jax.random.fold_in(jax.random.fold_in(arg_keys[5], part), 71), part),
        "doc_ids": jnp.searchsorted(jnp.cumsum(ragged_sizes(part_splits[2], DOCS, SLAB_TOKENS, DOCUMENT_LIMIT, 2)), jnp.arange(SLAB_TOKENS), side="right").astype(jnp.int32),
        "owner_tiles": draw_owner_tiles(jax.random.fold_in(jax.random.fold_in(arg_keys[5], part), 71), part),
        "tile_counts": draw_tile_counts(jax.random.fold_in(jax.random.fold_in(arg_keys[5], part), 71), part),
    }


def attend(queries, keys, value_rows, allowed):
    scale = HEAD_WIDTH ** -0.5
    scores = jnp.einsum("rhgd,khd->hgrk", queries.astype(jnp.float32), keys.astype(jnp.float32)) * scale
    scores = jnp.where(allowed[None, None], scores, -jnp.inf)
    row_top = jnp.max(scores, axis=3, keepdims=True)
    exponent = jnp.exp(scores - row_top)
    totals = jnp.sum(exponent, axis=3, keepdims=True)
    weights = exponent.astype(jnp.bfloat16)
    mixed_rows = jnp.einsum("hgrk,khd->rhgd", weights.astype(jnp.float32), value_rows.astype(jnp.float32))
    return (mixed_rows / jnp.transpose(totals, (2, 0, 1, 3))).astype(jnp.bfloat16)


def reference(queries, keyvalue, doc_ids, owner_tiles, tile_counts):
    group_width = QUERY_HEADS // KEY_VALUE_HEADS
    row_block = min(512, SLAB_TOKENS)
    query_heads = queries.reshape(SLAB_TOKENS, KEY_VALUE_HEADS, group_width, HEAD_WIDTH)
    keyvalue_heads = keyvalue.reshape(SLAB_TOKENS, KEY_VALUE_HEADS, 2, HEAD_WIDTH)
    padded_extent = jnp.zeros((DOCUMENT_LIMIT, KEY_VALUE_HEADS, 2, HEAD_WIDTH), keyvalue.dtype)
    kv_pad = jnp.concatenate([padded_extent, keyvalue_heads], axis=0)
    docs_pad = jnp.concatenate([jnp.full((DOCUMENT_LIMIT,), -1, jnp.int32), doc_ids.astype(jnp.int32)], axis=0)

    def one_block(block_id):
        begin_row = block_id * row_block
        q_block = lax.dynamic_slice_in_dim(query_heads, begin_row, row_block, 0)
        kv_block = lax.dynamic_slice_in_dim(kv_pad, begin_row, row_block + DOCUMENT_LIMIT, 0)
        q_docs = lax.dynamic_slice_in_dim(doc_ids.astype(jnp.int32), begin_row, row_block, 0)
        k_docs = lax.dynamic_slice_in_dim(docs_pad, begin_row, row_block + DOCUMENT_LIMIT, 0)
        q_place = jnp.arange(row_block, dtype=jnp.int32) + DOCUMENT_LIMIT
        k_place = jnp.arange(row_block + DOCUMENT_LIMIT, dtype=jnp.int32)
        allowed = (q_docs[:, None] == k_docs[None, :]) & (k_place[None, :] <= q_place[:, None])
        result = attend(q_block, kv_block[:, :, 0], kv_block[:, :, 1], allowed)
        return result.reshape(row_block, QUERY_HEADS * HEAD_WIDTH)

    attended = lax.map(one_block, jnp.arange(SLAB_TOKENS // row_block, dtype=jnp.int32)).reshape(SLAB_TOKENS, QUERY_HEADS * HEAD_WIDTH)
    tiles = attended.reshape(NTILE, TILE, QUERY_HEADS * HEAD_WIDTH)
    picked = jnp.take(tiles, owner_tiles.reshape(-1).astype(jnp.int32), axis=0)
    live = (jnp.arange(CAP, dtype=jnp.int32)[None, :] < tile_counts[:, None]).reshape(-1)
    owned = jnp.where(live[:, None, None], picked, jnp.zeros((), attended.dtype))
    return owned.reshape(N_SEQ * CAP * TILE, QUERY_HEADS * HEAD_WIDTH)
```

```python
import functools
import math

import jax
import jax.numpy as jnp
from jax import lax
from jax.experimental import pallas as pl
from jax.experimental.pallas import tpu as pltpu
from jax.sharding import PartitionSpec as P

QUERY_HEADS = 64
KEY_VALUE_HEADS = 8
HEAD_WIDTH = 128
TILE = 128
DOCUMENT_LIMIT = 512
GROUP = QUERY_HEADS // KEY_VALUE_HEADS
GROUP_COLS = GROUP * HEAD_WIDTH
MARK_COLS = 128
CORES = 2
STACK = 4
FIRST_GROUPS = 2
MASKED = -1e30


def shifted(block, by):
    count = lax.axis_size("seq")
    return lax.ppermute(block, "seq", [(i, i + by) for i in range(count - by)])


def to_sibling(block, senders):
    count = lax.axis_size("seq")
    pairs = [(i, i ^ 1) for i in range(count) if i % CORES in senders]
    return lax.ppermute(block, "seq", pairs)


def attend_kernel(blocks, core_ref, q_ref, doc_ref, *refs):
    given = blocks + 1
    kv_refs, mark_refs = refs[:given], refs[given : 2 * given]
    out_ref, bias = refs[2 * given :]
    rows = q_ref.shape[0]
    first_core = core_ref[0] == 0

    def in_use(entries):
        return [jnp.where(first_core, entries[0], entries[1])] + entries[2:]

    @pl.when(pl.program_id(0) == 0)
    def _():
        mine = doc_ref[...]
        marks = in_use([r[...].astype(jnp.float32) for r in mark_refs])
        for b in range(blocks):
            same = mine == marks[b][0:1, :]
            if b == blocks - 1:
                q_place = lax.broadcasted_iota(jnp.int32, (rows, rows), 0)
                k_place = lax.broadcasted_iota(jnp.int32, (rows, rows), 1)
                same = same & (k_place <= q_place)
            bias[:, b * rows : (b + 1) * rows] = jnp.where(same, 0.0, MASKED)

    keys = jnp.concatenate(in_use([r[:, :HEAD_WIDTH] for r in kv_refs]), axis=0)
    values = jnp.concatenate(in_use([r[:, HEAD_WIDTH:] for r in kv_refs]), axis=0)
    rate = HEAD_WIDTH**-0.5 * math.log2(math.e)
    for h in range(0, GROUP, STACK):
        q = jnp.concatenate(
            [q_ref[:, (h + i) * HEAD_WIDTH : (h + i + 1) * HEAD_WIDTH] for i in range(STACK)], axis=0
        )
        scores = lax.dot_general(q, keys, (((1,), (1,)), ((), ())), preferred_element_type=jnp.float32)
        scores = scores.reshape(STACK, rows, blocks * rows) + bias[...][None]
        top = jnp.max(scores, axis=2, keepdims=True)
        exponent = jnp.exp2((scores - top) * rate)
        totals = jnp.sum(exponent, axis=2, keepdims=True)
        weights = exponent.astype(jnp.bfloat16).reshape(STACK * rows, blocks * rows)
        mixed = jnp.dot(weights, values, preferred_element_type=jnp.float32)
        mixed = (mixed.reshape(STACK, rows, HEAD_WIDTH) / totals).astype(jnp.bfloat16)
        for i in range(STACK):
            out_ref[:, (h + i) * HEAD_WIDTH : (h + i + 1) * HEAD_WIDTH] = mixed[i]


def attend(core, queries, doc_rows, window, first, last):
    rows = queries.shape[0]
    blocks = len(window) - 1
    return pl.pallas_call(
        functools.partial(attend_kernel, blocks),
        grid=(last - first,),
        in_specs=[
            pl.BlockSpec(memory_space=pltpu.SMEM),
            pl.BlockSpec((rows, GROUP_COLS), lambda g: (0, g + first)),
            pl.BlockSpec((rows, MARK_COLS), lambda g: (0, 0)),
        ]
        + [pl.BlockSpec((rows, 2 * HEAD_WIDTH), lambda g: (0, g + first))] * len(window)
        + [pl.BlockSpec((16, MARK_COLS), lambda g: (0, 2 * KEY_VALUE_HEADS * HEAD_WIDTH // MARK_COLS))]
        * len(window),
        out_specs=pl.BlockSpec((rows, GROUP_COLS), lambda g: (0, g)),
        out_shape=jax.ShapeDtypeStruct((rows, (last - first) * GROUP_COLS), jnp.bfloat16),
        scratch_shapes=[pltpu.VMEM((rows, blocks * rows), jnp.float32)],
        compiler_params=pltpu.CompilerParams(vmem_limit_bytes=32 * 1024 * 1024),
        cost_estimate=pl.CostEstimate(
            flops=4 * (last - first) * GROUP_COLS * rows * rows * blocks,
            bytes_accessed=rows * (last - first) * (4 * GROUP_COLS + 4 * HEAD_WIDTH * blocks),
            transcendentals=(last - first) * GROUP * rows * rows * blocks,
        ),
    )(core, queries, doc_rows, *window, *window)


def place_kernel(parts, pick_ref, *refs):
    own, got = refs[:parts], refs[parts : 2 * parts]
    out_ref, blank, sems = refs[2 * parts :]
    rows = own[0].shape[0]
    slots = out_ref.shape[0] // rows
    blank[...] = jnp.zeros_like(blank)
    widths = [r.shape[1] for r in own]
    starts = [sum(widths[:i]) for i in range(parts)]

    def copies(slot, source):
        made = []
        for i in range(parts):
            if source is None:
                for c in range(0, widths[i], blank.shape[1]):
                    there = out_ref.at[pl.ds(slot * rows, rows), pl.ds(starts[i] + c, blank.shape[1])]
                    made.append(pltpu.make_async_copy(blank, there, sems.at[slot]))
            else:
                there = out_ref.at[pl.ds(slot * rows, rows), pl.ds(starts[i], widths[i])]
                made.append(pltpu.make_async_copy(source[i], there, sems.at[slot]))
        return made

    for step in ("start", "wait"):
        for slot in range(slots):
            for kind, source in enumerate((None, own, got)):

                @pl.when(pick_ref[slot] == kind)
                def _(slot=slot, source=source):
                    for copy in copies(slot, source):
                        getattr(copy, step)()


def place(pick, own, got):
    rows = own[0].shape[0]
    width = sum(o.shape[1] for o in own)
    return pl.pallas_call(
        functools.partial(place_kernel, len(own)),
        in_specs=[pl.BlockSpec(memory_space=pltpu.SMEM)]
        + [pl.BlockSpec(memory_space=pl.ANY)] * (2 * len(own)),
        out_specs=pl.BlockSpec(memory_space=pl.ANY),
        out_shape=jax.ShapeDtypeStruct((pick.shape[0] * rows, width), jnp.bfloat16),
        scratch_shapes=[pltpu.VMEM((rows, GROUP_COLS), jnp.bfloat16), pltpu.SemaphoreType.DMA((pick.shape[0],))],
    )(pick, *own, *got)


def local(queries, keyvalue, doc_ids, owner_tiles, tile_counts):
    count = lax.axis_size("seq")
    me = lax.axis_index("seq")
    rows = queries.shape[0]
    half = count // 2
    core = me % CORES
    back = (DOCUMENT_LIMIT - 1) // rows + 1

    doc_marks = (doc_ids + 1).astype(jnp.bfloat16)
    sent = jnp.concatenate([keyvalue, jnp.broadcast_to(doc_marks[None, :], (rows, rows))], axis=1)
    chips = [sent] + [shifted(sent, CORES * hop) for hop in range(1, back // CORES + 1)]
    other = [
        to_sibling(block, [0] if hop == 0 else [1] if CORES * hop == back else [0, 1])
        for hop, block in enumerate(chips)
    ]
    window = [other[-1], other[0], *other[1:-1], *chips[1:], sent]
    core = core.reshape(1)
    doc_rows = jnp.broadcast_to((doc_ids + 1).astype(jnp.float32)[:, None], (rows, MARK_COLS))

    spans = ((0, FIRST_GROUPS), (FIRST_GROUPS, KEY_VALUE_HEADS))
    up = [(i, i + half) for i in range(half)]
    down = [(i + half, i) for i in range(half)]

    def moving(pairs):
        def branch(core, queries, doc_rows, *window):
            own, got = [], []
            for first, last in spans:
                part = attend(core, queries, doc_rows, window, first, last)
                own.append(part)
                got.append(lax.ppermute(part, "seq", pairs) if pairs else part)
            return tuple(own), tuple(got)

        return branch

    held = tile_counts[0]
    lower = me < half
    first_tile = owner_tiles[0, 0]
    mode = jnp.where(
        held == 1,
        jnp.where(first_tile == me, 0, 3),
        jnp.where((held == 0) == lower, 1, 2),
    )
    own, got = lax.switch(
        mode, [moving(None), moving(up), moving(down), moving(up + down)], core, queries, doc_rows, *window
    )
    slot = jnp.arange(owner_tiles.shape[1], dtype=jnp.int32)
    pick = jnp.where(slot < held, jnp.where(owner_tiles[0] == me, 1, 2), 0).astype(jnp.int32)
    return place(pick, own, got)


def solution(mesh):
    placed = (
        P(("groups", "seq"), None),
        P(("groups", "seq"), None),
        P(("groups", "seq")),
        P(("groups", "seq"), None),
        P(("groups", "seq")),
    )
    return jax.shard_map(
        local, mesh=mesh, in_specs=placed, out_specs=P(("groups", "seq"), None), check_vma=False
    )
```

```python
import functools
import math

import jax
import jax.numpy as jnp
from jax import lax
from jax.experimental import pallas as pl
from jax.experimental.pallas import tpu as pltpu
from jax.sharding import PartitionSpec as P

QUERY_HEADS = 64
KEY_VALUE_HEADS = 8
HEAD_WIDTH = 128
TILE = 128
DOCUMENT_LIMIT = 512
GROUP = QUERY_HEADS // KEY_VALUE_HEADS
GROUP_COLS = GROUP * HEAD_WIDTH
MARK_COLS = 128
CORES = 2
STACK = 4
FIRST_GROUPS = 2
MASKED = -1e30


def shifted(block, by):
    count = lax.axis_size("seq")
    return lax.ppermute(block, "seq", [(i, i + by) for i in range(count - by)])


def to_sibling(block, senders):
    count = lax.axis_size("seq")
    pairs = [(i, i ^ 1) for i in range(count) if i % CORES in senders]
    return lax.ppermute(block, "seq", pairs)


def attend_kernel(blocks, core_ref, q_ref, doc_ref, *refs):
    given = blocks + 1
    kv_refs, mark_refs = refs[:given], refs[given : 2 * given]
    out_ref, bias = refs[2 * given :]
    rows = q_ref.shape[0]
    first_core = core_ref[0] == 0

    def in_use(entries):
        return [jnp.where(first_core, entries[0], entries[1])] + entries[2:]

    @pl.when(pl.program_id(0) == 0)
    def _():
        mine = doc_ref[...]
        marks = in_use([r[...].astype(jnp.float32) for r in mark_refs])
        for b in range(blocks):
            same = mine == marks[b][0:1, :]
            if b == blocks - 1:
                q_place = lax.broadcasted_iota(jnp.int32, (rows, rows), 0)
                k_place = lax.broadcasted_iota(jnp.int32, (rows, rows), 1)
                same = same & (k_place <= q_place)
            bias[:, b * rows : (b + 1) * rows] = jnp.where(same, 0.0, MASKED)

    keys = jnp.concatenate(in_use([r[:, :HEAD_WIDTH] for r in kv_refs]), axis=0)
    values = jnp.concatenate(in_use([r[:, HEAD_WIDTH:] for r in kv_refs]), axis=0)
    rate = HEAD_WIDTH**-0.5 * math.log2(math.e)
    for h in range(0, GROUP, STACK):
        q = jnp.concatenate(
            [q_ref[:, (h + i) * HEAD_WIDTH : (h + i + 1) * HEAD_WIDTH] for i in range(STACK)], axis=0
        )
        scores = lax.dot_general(q, keys, (((1,), (1,)), ((), ())), preferred_element_type=jnp.float32)
        scores = scores.reshape(STACK, rows, blocks * rows) + bias[...][None]
        top = jnp.max(scores, axis=2, keepdims=True)
        exponent = jnp.exp2((scores - top) * rate)
        totals = jnp.sum(exponent, axis=2, keepdims=True)
        weights = exponent.astype(jnp.bfloat16).reshape(STACK * rows, blocks * rows)
        mixed = jnp.dot(weights, values, preferred_element_type=jnp.float32)
        mixed = (mixed.reshape(STACK, rows, HEAD_WIDTH) / totals).astype(jnp.bfloat16)
        for i in range(STACK):
            out_ref[:, (h + i) * HEAD_WIDTH : (h + i + 1) * HEAD_WIDTH] = mixed[i]


def attend(core, queries, doc_rows, window, first, last):
    rows = queries.shape[0]
    blocks = len(window) - 1
    return pl.pallas_call(
        functools.partial(attend_kernel, blocks),
        grid=(last - first,),
        in_specs=[
            pl.BlockSpec(memory_space=pltpu.SMEM),
            pl.BlockSpec((rows, GROUP_COLS), lambda g: (0, g + first)),
            pl.BlockSpec((rows, MARK_COLS), lambda g: (0, 0)),
        ]
        + [pl.BlockSpec((rows, 2 * HEAD_WIDTH), lambda g: (0, g + first))] * len(window)
        + [pl.BlockSpec((16, MARK_COLS), lambda g: (0, 2 * KEY_VALUE_HEADS * HEAD_WIDTH // MARK_COLS))]
        * len(window),
        out_specs=pl.BlockSpec((rows, GROUP_COLS), lambda g: (0, g)),
        out_shape=jax.ShapeDtypeStruct((rows, (last - first) * GROUP_COLS), jnp.bfloat16),
        scratch_shapes=[pltpu.VMEM((rows, blocks * rows), jnp.float32)],
        compiler_params=pltpu.CompilerParams(vmem_limit_bytes=32 * 1024 * 1024),
        cost_estimate=pl.CostEstimate(
            flops=4 * (last - first) * GROUP_COLS * rows * rows * blocks,
            bytes_accessed=rows * (last - first) * (4 * GROUP_COLS + 4 * HEAD_WIDTH * blocks),
            transcendentals=(last - first) * GROUP * rows * rows * blocks,
        ),
    )(core, queries, doc_rows, *window, *window)


def place_kernel(spans, pick_ref, *refs):
    parts = len(spans)
    out_ref = refs[2 * parts]
    kind, step = pick_ref[pl.program_id(0)], pl.program_id(1)

    @pl.when(kind == 0)
    def _():
        out_ref[...] = jnp.zeros_like(out_ref)

    for i, (first, last) in enumerate(spans):
        inside = (step >= first) & (step < last)
        for source, ref in ((1, refs[i]), (2, refs[parts + i])):

            @pl.when(inside & (kind == source))
            def _(ref=ref):
                out_ref[...] = ref[...]


def place(pick, own, got, step_cols):
    rows = own[0].shape[0]
    widths = [o.shape[1] // step_cols for o in own]
    spans = [(sum(widths[:i]), sum(widths[: i + 1])) for i in range(len(own))]

    def block_of(source, first, last):
        def index(slot, step, pick_ref):
            return 0, jnp.where(pick_ref[slot] == source, jnp.clip(step - first, 0, last - first - 1), 0)

        return pl.BlockSpec((rows, step_cols), index)

    return pl.pallas_call(
        functools.partial(place_kernel, spans),
        grid_spec=pltpu.PrefetchScalarGridSpec(
            num_scalar_prefetch=1,
            grid=(pick.shape[0], spans[-1][1]),
            in_specs=[block_of(source, *span) for source in (1, 2) for span in spans],
            out_specs=pl.BlockSpec((rows, step_cols), lambda slot, step, pick_ref: (slot, step)),
        ),
        out_shape=jax.ShapeDtypeStruct((pick.shape[0] * rows, spans[-1][1] * step_cols), jnp.bfloat16),
    )(pick, *own, *got)


def local(queries, keyvalue, doc_ids, owner_tiles, tile_counts):
    count = lax.axis_size("seq")
    me = lax.axis_index("seq")
    rows = queries.shape[0]
    half = count // 2
    core = me % CORES
    back = (DOCUMENT_LIMIT - 1) // rows + 1

    doc_marks = (doc_ids + 1).astype(jnp.bfloat16)
    sent = jnp.concatenate([keyvalue, jnp.broadcast_to(doc_marks[None, :], (rows, rows))], axis=1)
    chips = [sent] + [shifted(sent, CORES * hop) for hop in range(1, back // CORES + 1)]
    other = [
        to_sibling(block, [0] if hop == 0 else [1] if CORES * hop == back else [0, 1])
        for hop, block in enumerate(chips)
    ]
    window = [other[-1], other[0], *other[1:-1], *chips[1:], sent]
    core = core.reshape(1)
    doc_rows = jnp.broadcast_to((doc_ids + 1).astype(jnp.float32)[:, None], (rows, MARK_COLS))

    spans = ((0, FIRST_GROUPS), (FIRST_GROUPS, KEY_VALUE_HEADS))
    up = [(i, i + half) for i in range(half)]
    down = [(i + half, i) for i in range(half)]

    def moving(pairs):
        def branch(core, queries, doc_rows, *window):
            own, got = [], []
            for first, last in spans:
                part = attend(core, queries, doc_rows, window, first, last)
                own.append(part)
                got.append(lax.ppermute(part, "seq", pairs) if pairs else part)
            return tuple(own), tuple(got)

        return branch

    held = tile_counts[0]
    lower = me < half
    first_tile = owner_tiles[0, 0]
    mode = jnp.where(
        held == 1,
        jnp.where(first_tile == me, 0, 3),
        jnp.where((held == 0) == lower, 1, 2),
    )
    own, got = lax.switch(
        mode, [moving(None), moving(up), moving(down), moving(up + down)], core, queries, doc_rows, *window
    )
    slot = jnp.arange(owner_tiles.shape[1], dtype=jnp.int32)
    pick = jnp.where(slot < held, jnp.where(owner_tiles[0] == me, 1, 2), 0).astype(jnp.int32)
    return place(pick, own, got, FIRST_GROUPS * GROUP_COLS)


def solution(mesh):
    placed = (
        P(("groups", "seq"), None),
        P(("groups", "seq"), None),
        P(("groups", "seq")),
        P(("groups", "seq"), None),
        P(("groups", "seq")),
    )
    return jax.shard_map(
        local, mesh=mesh, in_specs=placed, out_specs=P(("groups", "seq"), None), check_vma=False
    )
```

```python
import functools
import math

import jax
import jax.numpy as jnp
from jax import lax
from jax.experimental import pallas as pl
from jax.experimental.pallas import tpu as pltpu
from jax.sharding import PartitionSpec as P

QUERY_HEADS = 64
KEY_VALUE_HEADS = 8
HEAD_WIDTH = 128
TILE = 128
DOCUMENT_LIMIT = 512
GROUP = QUERY_HEADS // KEY_VALUE_HEADS
GROUP_COLS = GROUP * HEAD_WIDTH
MARK_COLS = 128
CORES = 2
STACK = 4
SPANS = ((0, 3), (3, 6), (6, 8))
MASKED = -1e30
IN_HBM = pl.BlockSpec(memory_space=pltpu.HBM)


def send(block, pairs):
    return lax.ppermute(block, "seq", pairs)


def mark_rows(ref):
    return ref[0:1, :].astype(jnp.float32)


def attend_kernel(first, span, given, chained, core_ref, pick_ref, q_hbm, mine_ref, *refs):
    blocks = given - 1
    kv_refs, mark_refs = refs[:given], refs[given : 2 * given - 1]
    scratch = refs[2 * given - 1 + chained :]
    part_ref, out_ref, q_buf, kv_buf, o_buf, blank, bias, q_sems, kv_sems, o_sems, blank_sems = scratch
    rows = q_buf.shape[1]
    slots = pick_ref.shape[0]
    all_keys = blocks * rows
    rate = HEAD_WIDTH**-0.5 * math.log2(math.e)

    def cols_of(g, width):
        return pl.ds(pl.multiple_of(g * width, width), width)

    def arriving(g, step):
        turn = lax.rem(g, 2)
        copy = pltpu.make_async_copy(
            q_hbm.at[:, cols_of(first + g, GROUP_COLS)], q_buf.at[turn], q_sems.at[turn]
        )
        getattr(copy, step)()

        def block(i, b):
            copy = pltpu.make_async_copy(
                kv_refs[i].at[:, cols_of(first + g, 2 * HEAD_WIDTH)],
                kv_buf.at[turn, pl.ds(b * rows, rows), :],
                kv_sems.at[turn, b],
            )
            getattr(copy, step)()

        pl.when(core_ref[0] == 0)(lambda: block(0, 0))
        pl.when(core_ref[0] != 0)(lambda: block(1, 0))
        for b in range(1, blocks):
            block(b + 1, b)

    def leaving(g, step):
        turn = lax.rem(g, 2)
        copy = pltpu.make_async_copy(o_buf.at[turn], part_ref.at[:, cols_of(g, GROUP_COLS)], o_sems.at[turn, slots])
        getattr(copy, step)()
        for slot in range(slots):
            there = out_ref.at[pl.ds(slot * rows, rows), cols_of(first + g, GROUP_COLS)]
            copy = pltpu.make_async_copy(o_buf.at[turn], there, o_sems.at[turn, slot])
            pl.when(pick_ref[slot] == 1)(getattr(copy, step))

    def clearing(step):
        for slot in range(slots):

            @pl.when(pick_ref[slot] == 0)
            def _(slot=slot):
                for g in range(span):
                    there = out_ref.at[pl.ds(slot * rows, rows), pl.ds((first + g) * GROUP_COLS, GROUP_COLS)]
                    getattr(pltpu.make_async_copy(blank, there, blank_sems.at[slot, g]), step)()

    arriving(0, "start")
    blank[...] = jnp.zeros_like(blank)
    clearing("start")

    marks = [jnp.where(core_ref[0] == 0, mark_rows(mark_refs[0]), mark_rows(mark_refs[1]))]
    marks += [mark_rows(r) for r in (*mark_refs[2:], mine_ref)]
    mine = mine_ref[...].astype(jnp.float32).T
    for b, theirs in enumerate(marks):
        same = mine == theirs
        if b == blocks - 1:
            q_place = lax.broadcasted_iota(jnp.int32, (rows, rows), 0)
            k_place = lax.broadcasted_iota(jnp.int32, (rows, rows), 1)
            same = same & (k_place <= q_place)
        bias[:, b * rows : (b + 1) * rows] = jnp.where(same, 0.0, MASKED)

    def one_group(g, carry):
        turn = lax.rem(g, 2)
        pl.when(g + 1 < span)(lambda: arriving(g + 1, "start"))
        arriving(g, "wait")
        pl.when(g >= 2)(lambda: leaving(g - 2, "wait"))
        keys, values = kv_buf[turn, :, :HEAD_WIDTH], kv_buf[turn, :, HEAD_WIDTH:]
        for h in range(0, GROUP, STACK):
            q = jnp.concatenate(
                [q_buf[turn, :, (h + i) * HEAD_WIDTH : (h + i + 1) * HEAD_WIDTH] for i in range(STACK)], axis=0
            )
            scores = lax.dot_general(q, keys, (((1,), (1,)), ((), ())), preferred_element_type=jnp.float32)
            scores = scores.reshape(STACK, rows, all_keys) + bias[...][None]
            top = jnp.max(scores, axis=2, keepdims=True)
            exponent = jnp.exp2((scores - top) * rate)
            totals = jnp.sum(exponent, axis=2, keepdims=True)
            weights = exponent.astype(jnp.bfloat16).reshape(STACK * rows, all_keys)
            mixed = jnp.dot(weights, values, preferred_element_type=jnp.float32)
            mixed = (mixed.reshape(STACK, rows, HEAD_WIDTH) / totals).astype(jnp.bfloat16)
            for i in range(STACK):
                o_buf[turn, :, (h + i) * HEAD_WIDTH : (h + i + 1) * HEAD_WIDTH] = mixed[i]
        leaving(g, "start")
        return carry

    lax.fori_loop(0, span, one_group, 0)
    for g in range(max(span - 2, 0), span):
        leaving(g, "wait")
    clearing("wait")


def attend(core, pick, queries, window, out, first, last):
    rows, width = queries.shape
    span = last - first
    slots = pick.shape[0]
    blocks = len(window) - 1
    chained = [] if out is None else [out]
    anywhere = pl.BlockSpec(memory_space=pl.ANY)

    def mark_spec(array, count):
        block = array.shape[1] // MARK_COLS - 1
        return pl.BlockSpec((count, MARK_COLS), lambda i: (0, block))

    return pl.pallas_call(
        functools.partial(attend_kernel, first, span, len(window), len(chained)),
        grid=(1,),
        in_specs=[pl.BlockSpec(memory_space=pltpu.SMEM)] * 2
        + [anywhere, mark_spec(window[-1], rows)]
        + [anywhere] * len(window)
        + [mark_spec(w, 16) for w in window[:-1]]
        + [IN_HBM] * len(chained),
        out_specs=[anywhere, IN_HBM],
        out_shape=[
            jax.ShapeDtypeStruct((rows, span * GROUP_COLS), jnp.bfloat16),
            pltpu.HBM((slots * rows, width), jnp.bfloat16),
        ],
        input_output_aliases={3 + 2 * len(window): 1} if chained else {},
        scratch_shapes=[
            pltpu.VMEM((2, rows, GROUP_COLS), jnp.bfloat16),
            pltpu.VMEM((2, blocks * rows, 2 * HEAD_WIDTH), jnp.bfloat16),
            pltpu.VMEM((2, rows, GROUP_COLS), jnp.bfloat16),
            pltpu.VMEM((rows, GROUP_COLS), jnp.bfloat16),
            pltpu.VMEM((rows, blocks * rows), jnp.float32),
            pltpu.SemaphoreType.DMA((2,)),
            pltpu.SemaphoreType.DMA((2, blocks)),
            pltpu.SemaphoreType.DMA((2, slots + 1)),
            pltpu.SemaphoreType.DMA((slots, span)),
        ],
        compiler_params=pltpu.CompilerParams(vmem_limit_bytes=24 * 1024 * 1024),
        cost_estimate=pl.CostEstimate(flops=0, bytes_accessed=0, transcendentals=0),
    )(core, pick, queries, window[-1], *window, *window[:-1], *chained)


def deliver_kernel(starts, pick_ref, *refs):
    got = refs[: len(starts)]
    out_ref, sems = refs[len(starts) + 1 :]
    rows = got[0].shape[0]
    for slot in range(pick_ref.shape[0]):

        @pl.when(pick_ref[slot] == 2)
        def _(slot=slot):
            copies = [
                pltpu.make_async_copy(
                    ref, out_ref.at[pl.ds(slot * rows, rows), pl.ds(c, ref.shape[1])], sems.at[i]
                )
                for i, (ref, c) in enumerate(zip(got, starts))
            ]
            for copy in copies:
                copy.start()
            for copy in copies:
                copy.wait()


def deliver(pick, got, starts, out):
    return pl.pallas_call(
        functools.partial(deliver_kernel, starts),
        grid=(1,),
        in_specs=[pl.BlockSpec(memory_space=pltpu.SMEM)]
        + [pl.BlockSpec(g.shape, lambda i: (0, 0)) for g in got]
        + [IN_HBM],
        out_specs=IN_HBM,
        out_shape=pltpu.HBM(out.shape, out.dtype),
        input_output_aliases={1 + len(got): 0},
        scratch_shapes=[pltpu.SemaphoreType.DMA((len(got),))],
        compiler_params=pltpu.CompilerParams(vmem_limit_bytes=24 * 1024 * 1024),
    )(pick, *got, out)


def local(queries, keyvalue, doc_ids, owner_tiles, tile_counts):
    count = lax.axis_size("seq")
    me = lax.axis_index("seq")
    rows = queries.shape[0]
    half = count // 2

    far = [(i, i + 2 * CORES) for i in range(count - 2 * CORES)]
    near = [(i, i + CORES) for i in range(count - CORES)]
    cross = [(i, i ^ 1) for i in range(count)]
    marks = jnp.broadcast_to((doc_ids + 1).astype(jnp.bfloat16)[None, :], (rows, MARK_COLS))
    sent = jnp.concatenate([keyvalue, marks], axis=1)
    far_block = send(sent, far)
    near_block = send(sent, near)
    own_crossed = send(sent, [p for p in cross if p[0] % CORES == 0])

    held = tile_counts[0]
    slot = jnp.arange(owner_tiles.shape[1], dtype=jnp.int32)
    pick = jnp.where(slot < held, jnp.where(owner_tiles[0] == me, 1, 2), 0).astype(jnp.int32)
    mode = jnp.where(
        held == 1,
        jnp.where(owner_tiles[0, 0] == me, 0, 3),
        jnp.where((held == 0) == (me < half), 1, 2),
    )
    core = (me % CORES).reshape(1)
    near_block, pick, mode, core = lax.optimization_barrier((near_block, pick, mode, core))

    far_crossed = send(far_block, [p for p in cross if p[0] % CORES == 1])
    near_crossed = send(near_block, cross)
    window = [far_crossed, own_crossed, near_crossed, near_block, far_block, sent]
    part, out = attend(core, pick, queries, window, None, *SPANS[0])

    up = [(i, i + half) for i in range(half)]
    down = [(i + half, i) for i in range(half)]
    starts = [first * GROUP_COLS for first, _ in SPANS]

    def moving(pairs):
        def branch(core, pick, queries, part, out, window):
            got = []
            for first, last in SPANS[1:]:
                if pairs:
                    got.append(send(part, pairs))
                part, out = attend(core, pick, queries, window, out, first, last)
            if pairs:
                got.append(send(part, pairs))
                for part, start in zip(got, starts):
                    out = deliver(pick, [part], [start], out)
            return out

        return branch

    branches = [moving(None), moving(up), moving(down), moving(up + down)]
    return lax.switch(mode, branches, core, pick, queries, part, out, window)


def solution(mesh):
    placed = (
        P(("groups", "seq"), None),
        P(("groups", "seq"), None),
        P(("groups", "seq")),
        P(("groups", "seq"), None),
        P(("groups", "seq")),
    )
    return jax.shard_map(
        local, mesh=mesh, in_specs=placed, out_specs=P(("groups", "seq"), None), check_vma=False
    )
```

```python
import functools
import math

import jax
import jax.numpy as jnp
from jax import lax
from jax.experimental import pallas as pl
from jax.experimental.pallas import tpu as pltpu
from jax.sharding import PartitionSpec as P

QUERY_HEADS = 64
KEY_VALUE_HEADS = 8
HEAD_WIDTH = 128
TILE = 128
DOCUMENT_LIMIT = 512
GROUP = QUERY_HEADS // KEY_VALUE_HEADS
GROUP_COLS = GROUP * HEAD_WIDTH
MARK_COLS = 128
CORES = 2
STACK = 4
SPANS = ((0, 3), (3, 6), (6, 8))
MASKED = -1e30
IN_HBM = pl.BlockSpec(memory_space=pltpu.HBM)


def send(block, pairs):
    return lax.ppermute(block, "seq", pairs)


def mark_kernel(doc_ref, kv_ref, out_ref):
    rows, cols = kv_ref.shape
    out_ref[:, :cols] = kv_ref[...]
    marks = (doc_ref[...] + 1).astype(jnp.float32)
    out_ref[:, cols:] = jnp.broadcast_to(marks, (rows, MARK_COLS)).astype(jnp.bfloat16)


def mark(keyvalue, doc_ids, cols):
    rows = keyvalue.shape[0]
    return pl.pallas_call(
        mark_kernel,
        grid=(1,),
        in_specs=[pl.BlockSpec((1, rows), lambda i: (0, 0)), pl.BlockSpec((rows, cols), lambda i: (0, 0))],
        out_specs=pl.BlockSpec((rows, cols + MARK_COLS), lambda i: (0, 0)),
        out_shape=jax.ShapeDtypeStruct((rows, cols + MARK_COLS), jnp.bfloat16),
    )(doc_ids.reshape(1, rows), keyvalue)


def mark_rows(ref):
    return ref[0:1, :].astype(jnp.float32)


def attend_kernel(first, span, offset, given, chained, core_ref, pick_ref, q_hbm, mine_ref, *refs):
    blocks = given - 1
    kv_refs, mark_refs = refs[:given], refs[given : 2 * given - 1]
    scratch = refs[2 * given - 1 + chained :]
    part_ref, out_ref, q_buf, kv_buf, o_buf, blank, bias, q_sems, kv_sems, o_sems, blank_sems = scratch
    rows = q_buf.shape[1]
    slots = pick_ref.shape[0]
    all_keys = blocks * rows
    rate = HEAD_WIDTH**-0.5 * math.log2(math.e)

    def cols_of(g, width):
        return pl.ds(pl.multiple_of(g * width, width), width)

    def arriving(g, step):
        turn = lax.rem(g, 2)
        copy = pltpu.make_async_copy(
            q_hbm.at[:, cols_of(first + g, GROUP_COLS)], q_buf.at[turn], q_sems.at[turn]
        )
        getattr(copy, step)()

        def block(i, b):
            copy = pltpu.make_async_copy(
                kv_refs[i].at[:, cols_of(first - offset + g, 2 * HEAD_WIDTH)],
                kv_buf.at[turn, pl.ds(b * rows, rows), :],
                kv_sems.at[turn, b],
            )
            getattr(copy, step)()

        pl.when(core_ref[0] == 0)(lambda: block(0, 0))
        pl.when(core_ref[0] != 0)(lambda: block(1, 0))
        for b in range(1, blocks):
            block(b + 1, b)

    def leaving(g, step):
        turn = lax.rem(g, 2)
        copy = pltpu.make_async_copy(o_buf.at[turn], part_ref.at[:, cols_of(g, GROUP_COLS)], o_sems.at[turn, slots])
        getattr(copy, step)()
        for slot in range(slots):
            there = out_ref.at[pl.ds(slot * rows, rows), cols_of(first + g, GROUP_COLS)]
            copy = pltpu.make_async_copy(o_buf.at[turn], there, o_sems.at[turn, slot])
            pl.when(pick_ref[slot] == 1)(getattr(copy, step))

    def clearing(step):
        for slot in range(slots):

            @pl.when(pick_ref[slot] == 0)
            def _(slot=slot):
                for g in range(span):
                    there = out_ref.at[pl.ds(slot * rows, rows), pl.ds((first + g) * GROUP_COLS, GROUP_COLS)]
                    getattr(pltpu.make_async_copy(blank, there, blank_sems.at[slot, g]), step)()

    arriving(0, "start")
    blank[...] = jnp.zeros_like(blank)
    clearing("start")

    marks = [jnp.where(core_ref[0] == 0, mark_rows(mark_refs[0]), mark_rows(mark_refs[1]))]
    marks += [mark_rows(r) for r in (*mark_refs[2:], mine_ref)]
    mine = mine_ref[...].astype(jnp.float32).T
    for b, theirs in enumerate(marks):
        same = mine == theirs
        if b == blocks - 1:
            q_place = lax.broadcasted_iota(jnp.int32, (rows, rows), 0)
            k_place = lax.broadcasted_iota(jnp.int32, (rows, rows), 1)
            same = same & (k_place <= q_place)
        bias[:, b * rows : (b + 1) * rows] = jnp.where(same, 0.0, MASKED)

    def one_group(g, carry):
        turn = lax.rem(g, 2)
        pl.when(g + 1 < span)(lambda: arriving(g + 1, "start"))
        arriving(g, "wait")
        pl.when(g >= 2)(lambda: leaving(g - 2, "wait"))
        keys, values = kv_buf[turn, :, :HEAD_WIDTH], kv_buf[turn, :, HEAD_WIDTH:]
        for h in range(0, GROUP, STACK):
            q = jnp.concatenate(
                [q_buf[turn, :, (h + i) * HEAD_WIDTH : (h + i + 1) * HEAD_WIDTH] for i in range(STACK)], axis=0
            )
            scores = lax.dot_general(q, keys, (((1,), (1,)), ((), ())), preferred_element_type=jnp.float32)
            scores = scores.reshape(STACK, rows, all_keys) + bias[...][None]
            top = jnp.max(scores, axis=2, keepdims=True)
            exponent = jnp.exp2((scores - top) * rate)
            totals = jnp.sum(exponent, axis=2, keepdims=True)
            weights = exponent.astype(jnp.bfloat16).reshape(STACK * rows, all_keys)
            mixed = jnp.dot(weights, values, preferred_element_type=jnp.float32)
            mixed = (mixed.reshape(STACK, rows, HEAD_WIDTH) / totals).astype(jnp.bfloat16)
            for i in range(STACK):
                o_buf[turn, :, (h + i) * HEAD_WIDTH : (h + i + 1) * HEAD_WIDTH] = mixed[i]
        leaving(g, "start")
        return carry

    lax.fori_loop(0, span, one_group, 0)
    for g in range(max(span - 2, 0), span):
        leaving(g, "wait")
    clearing("wait")


def attend(core, pick, queries, window, offset, marked, out, first, last):
    rows, width = queries.shape
    span = last - first
    slots = pick.shape[0]
    blocks = len(window) - 1
    chained = [] if out is None else [out]
    anywhere = pl.BlockSpec(memory_space=pl.ANY)

    def mark_spec(array, count):
        block = array.shape[1] // MARK_COLS - 1
        return pl.BlockSpec((count, MARK_COLS), lambda i: (0, block))

    return pl.pallas_call(
        functools.partial(attend_kernel, first, span, offset, len(window), len(chained)),
        grid=(1,),
        in_specs=[pl.BlockSpec(memory_space=pltpu.SMEM)] * 2
        + [anywhere, mark_spec(marked[-1], rows)]
        + [anywhere] * len(window)
        + [mark_spec(w, 16) for w in marked[:-1]]
        + [IN_HBM] * len(chained),
        out_specs=[anywhere, IN_HBM],
        out_shape=[
            jax.ShapeDtypeStruct((rows, span * GROUP_COLS), jnp.bfloat16),
            pltpu.HBM((slots * rows, width), jnp.bfloat16),
        ],
        input_output_aliases={3 + 2 * len(window): 1} if chained else {},
        scratch_shapes=[
            pltpu.VMEM((2, rows, GROUP_COLS), jnp.bfloat16),
            pltpu.VMEM((2, blocks * rows, 2 * HEAD_WIDTH), jnp.bfloat16),
            pltpu.VMEM((2, rows, GROUP_COLS), jnp.bfloat16),
            pltpu.VMEM((rows, GROUP_COLS), jnp.bfloat16),
            pltpu.VMEM((rows, blocks * rows), jnp.float32),
            pltpu.SemaphoreType.DMA((2,)),
            pltpu.SemaphoreType.DMA((2, blocks)),
            pltpu.SemaphoreType.DMA((2, slots + 1)),
            pltpu.SemaphoreType.DMA((slots, span)),
        ],
        compiler_params=pltpu.CompilerParams(vmem_limit_bytes=24 * 1024 * 1024),
        cost_estimate=pl.CostEstimate(flops=0, bytes_accessed=0, transcendentals=0),
    )(core, pick, queries, marked[-1], *window, *marked[:-1], *chained)


def deliver_kernel(starts, pick_ref, *refs):
    got = refs[: len(starts)]
    out_ref, sems = refs[len(starts) + 1 :]
    rows = got[0].shape[0]
    for slot in range(pick_ref.shape[0]):

        @pl.when(pick_ref[slot] == 2)
        def _(slot=slot):
            copies = [
                pltpu.make_async_copy(
                    ref, out_ref.at[pl.ds(slot * rows, rows), pl.ds(c, ref.shape[1])], sems.at[i]
                )
                for i, (ref, c) in enumerate(zip(got, starts))
            ]
            for copy in copies:
                copy.start()
            for copy in copies:
                copy.wait()


def deliver(pick, got, starts, out):
    return pl.pallas_call(
        functools.partial(deliver_kernel, starts),
        grid=(1,),
        in_specs=[pl.BlockSpec(memory_space=pltpu.SMEM)]
        + [pl.BlockSpec(g.shape, lambda i: (0, 0)) for g in got]
        + [IN_HBM],
        out_specs=IN_HBM,
        out_shape=pltpu.HBM(out.shape, out.dtype),
        input_output_aliases={1 + len(got): 0},
        scratch_shapes=[pltpu.SemaphoreType.DMA((len(got),))],
        compiler_params=pltpu.CompilerParams(vmem_limit_bytes=24 * 1024 * 1024),
    )(pick, *got, out)


def local(queries, keyvalue, doc_ids, owner_tiles, tile_counts):
    count = lax.axis_size("seq")
    me = lax.axis_index("seq")
    rows = queries.shape[0]
    half = count // 2

    far = [(i, i + 2 * CORES) for i in range(count - 2 * CORES)]
    near = [(i, i + CORES) for i in range(count - CORES)]
    cross = [(i, i ^ 1) for i in range(count)]
    cross_up = [p for p in cross if p[0] % CORES == 0]
    cross_down = [p for p in cross if p[0] % CORES == 1]
    split = SPANS[0][1]
    cut = split * 2 * HEAD_WIDTH
    marked = mark(keyvalue, doc_ids, cut)
    rest = keyvalue[:, cut:]
    far_early, near_early = send(marked, far), send(marked, near)
    far_late, near_late = send(rest, far), send(rest, near)
    own_early, own_late = send(marked, cross_up), send(rest, cross_up)

    held = tile_counts[0]
    slot = jnp.arange(owner_tiles.shape[1], dtype=jnp.int32)
    pick = jnp.where(slot < held, jnp.where(owner_tiles[0] == me, 1, 2), 0).astype(jnp.int32)
    mode = jnp.where(
        held == 1,
        jnp.where(owner_tiles[0, 0] == me, 0, 3),
        jnp.where((held == 0) == (me < half), 1, 2),
    )
    core = (me % CORES).reshape(1)
    near_early, pick, mode, core = lax.optimization_barrier((near_early, pick, mode, core))

    def window(far_block, near_block, own_crossed, own):
        return [send(far_block, cross_down), own_crossed, send(near_block, cross), near_block, far_block, own]

    early = window(far_early, near_early, own_early, marked)
    part, out = attend(core, pick, queries, early, 0, early, None, *SPANS[0])
    part, far_late, near_late = lax.optimization_barrier((part, far_late, near_late))
    late = window(far_late, near_late, own_late, rest)

    up = [(i, i + half) for i in range(half)]
    down = [(i + half, i) for i in range(half)]
    starts = [first * GROUP_COLS for first, _ in SPANS]

    def moving(pairs):
        def branch(core, pick, queries, part, out, early, late):
            got = []
            for first, last in SPANS[1:]:
                if pairs:
                    got.append(send(part, pairs))
                part, out = attend(core, pick, queries, late, split, early, out, first, last)
            if pairs:
                got.append(send(part, pairs))
                for part, start in zip(got, starts):
                    out = deliver(pick, [part], [start], out)
            return out

        return branch

    branches = [moving(None), moving(up), moving(down), moving(up + down)]
    return lax.switch(mode, branches, core, pick, queries, part, out, early, late)


def solution(mesh):
    placed = (
        P(("groups", "seq"), None),
        P(("groups", "seq"), None),
        P(("groups", "seq")),
        P(("groups", "seq"), None),
        P(("groups", "seq")),
    )
    return jax.shard_map(
        local, mesh=mesh, in_specs=placed, out_specs=P(("groups", "seq"), None), check_vma=False
    )
```

```python
import functools
import math

import jax
import jax.numpy as jnp
from jax import lax
from jax.experimental import pallas as pl
from jax.experimental.pallas import tpu as pltpu
from jax.sharding import PartitionSpec as P

QUERY_HEADS = 64
KEY_VALUE_HEADS = 8
HEAD_WIDTH = 128
TILE = 128
DOCUMENT_LIMIT = 512
GROUP = QUERY_HEADS // KEY_VALUE_HEADS
GROUP_COLS = GROUP * HEAD_WIDTH
MARK_COLS = 128
CORES = 2
STACK = 4
SPANS = ((0, 3), (3, 6), (6, 8))
MASKED = -1e30
IN_HBM = pl.BlockSpec(memory_space=pltpu.HBM)


def send(block, pairs):
    return lax.ppermute(block, "seq", pairs)


def prepare_kernel(doc_ref, kv_ref, tiles_ref, counts_ref, early_ref, late_ref, pick_ref, mode_ref):
    rows = kv_ref.shape[0]
    cut = early_ref.shape[1] - MARK_COLS
    marks = (doc_ref[...] + 1).astype(jnp.float32)
    early_ref[:, :cut] = kv_ref[:, :cut]
    early_ref[:, cut:] = jnp.broadcast_to(marks, (rows, MARK_COLS)).astype(jnp.bfloat16)
    late_ref[...] = kv_ref[:, cut:]
    me = lax.axis_index("seq")
    held = counts_ref[0]
    for slot in range(pick_ref.shape[0]):
        kind = jnp.where(tiles_ref[0, slot] == me, 1, 2)
        pick_ref[slot] = jnp.where(slot < held, kind, 0).astype(jnp.int32)
    lower = me < lax.axis_size("seq") // 2
    alone = jnp.where((held == 0) == lower, 1, 2)
    mode_ref[0] = jnp.where(held == 1, jnp.where(tiles_ref[0, 0] == me, 0, 3), alone).astype(jnp.int32)


def prepare(keyvalue, doc_ids, owner_tiles, tile_counts, cut):
    rows, cols = keyvalue.shape
    slots = owner_tiles.shape[1]
    scalars = pl.BlockSpec(memory_space=pltpu.SMEM)
    whole = [(rows, cut + MARK_COLS), (rows, cols - cut)]
    return pl.pallas_call(
        prepare_kernel,
        grid=(1,),
        in_specs=[pl.BlockSpec((1, rows), lambda i: (0, 0)), pl.BlockSpec((rows, cols), lambda i: (0, 0))]
        + [scalars] * 2,
        out_specs=[pl.BlockSpec(w, lambda i: (0, 0)) for w in whole] + [scalars] * 2,
        out_shape=[jax.ShapeDtypeStruct(w, jnp.bfloat16) for w in whole]
        + [jax.ShapeDtypeStruct((slots,), jnp.int32), jax.ShapeDtypeStruct((1,), jnp.int32)],
    )(doc_ids.reshape(1, rows), keyvalue, owner_tiles, tile_counts)


def attend_kernel(first, span, offset, chained, pick_ref, q_hbm, *refs):
    kv_refs, mark_refs = refs[:6], refs[6:12]
    scratch = refs[12 + chained :]
    part_ref, out_ref, q_buf, kv_buf, o_buf, blank, marks, bias, q_sems, kv_sems, o_sems, blank_sems, mark_sems = scratch
    rows = q_buf.shape[1]
    slots = pick_ref.shape[0]
    first_core = lax.axis_index("seq") % CORES == 0
    rate = HEAD_WIDTH**-0.5 * math.log2(math.e)
    mark_place = mark_refs[0].shape[1] - MARK_COLS

    def nearest_first(use):
        use(0, 5)
        pl.when(first_core)(lambda: use(1, 0))
        pl.when(jnp.logical_not(first_core))(lambda: use(1, 1))
        use(2, 2)
        pl.when(first_core)(lambda: use(3, 3))
        pl.when(jnp.logical_not(first_core))(lambda: use(3, 0))
        use(4, 4)

    def cols_of(g, width):
        return pl.ds(pl.multiple_of(g * width, width), width)

    def arriving(g, step):
        turn = lax.rem(g, 2)
        copy = pltpu.make_async_copy(
            q_hbm.at[:, cols_of(first + g, GROUP_COLS)], q_buf.at[turn], q_sems.at[turn]
        )
        getattr(copy, step)()

        def block(b, i):
            copy = pltpu.make_async_copy(
                kv_refs[i].at[:, cols_of(first - offset + g, 2 * HEAD_WIDTH)],
                kv_buf.at[turn, pl.ds(b * rows, rows), :],
                kv_sems.at[turn, b],
            )
            getattr(copy, step)()

        nearest_first(block)

    def reading_marks(step):
        def block(b, i):
            copy = pltpu.make_async_copy(
                mark_refs[i].at[pl.ds(0, rows), pl.ds(mark_place, MARK_COLS)], marks.at[b], mark_sems.at[b]
            )
            getattr(copy, step)()

        nearest_first(block)

    def leaving(g, step):
        turn = lax.rem(g, 2)
        copy = pltpu.make_async_copy(o_buf.at[turn], part_ref.at[:, cols_of(g, GROUP_COLS)], o_sems.at[turn, slots])
        getattr(copy, step)()
        for slot in range(slots):
            there = out_ref.at[pl.ds(slot * rows, rows), cols_of(first + g, GROUP_COLS)]
            copy = pltpu.make_async_copy(o_buf.at[turn], there, o_sems.at[turn, slot])
            pl.when(pick_ref[slot] == 1)(getattr(copy, step))

    def clearing(step):
        for slot in range(slots):

            @pl.when(pick_ref[slot] == 0)
            def _(slot=slot):
                for g in range(span):
                    there = out_ref.at[pl.ds(slot * rows, rows), pl.ds((first + g) * GROUP_COLS, GROUP_COLS)]
                    getattr(pltpu.make_async_copy(blank, there, blank_sems.at[slot, g]), step)()

    reading_marks("start")
    arriving(0, "start")
    blank[...] = jnp.zeros_like(blank)
    clearing("start")
    reading_marks("wait")
    mine = marks[0].astype(jnp.float32).T
    for b in range(marks.shape[0]):
        same = mine == marks[b, 0:1, :].astype(jnp.float32)
        if b == 0:
            q_place = lax.broadcasted_iota(jnp.int32, (rows, rows), 0)
            k_place = lax.broadcasted_iota(jnp.int32, (rows, rows), 1)
            same = same & (k_place <= q_place)
        bias[:, b * rows : (b + 1) * rows] = jnp.where(same, 0.0, MASKED)
    third = marks[3, 0:1, :].astype(jnp.float32)
    reaches = jnp.max(jnp.where(third == marks[0, 0:1, 0:1].astype(jnp.float32), 1.0, 0.0)) > 0.5

    def attention(blocks):
        held = blocks * rows

        def one_group(g, carry):
            turn = lax.rem(g, 2)
            pl.when(g + 1 < span)(lambda: arriving(g + 1, "start"))
            arriving(g, "wait")
            pl.when(g >= 2)(lambda: leaving(g - 2, "wait"))
            keys, values = kv_buf[turn, :held, :HEAD_WIDTH], kv_buf[turn, :held, HEAD_WIDTH:]
            for h in range(0, GROUP, STACK):
                q = jnp.concatenate(
                    [q_buf[turn, :, (h + i) * HEAD_WIDTH : (h + i + 1) * HEAD_WIDTH] for i in range(STACK)], axis=0
                )
                scores = lax.dot_general(q, keys, (((1,), (1,)), ((), ())), preferred_element_type=jnp.float32)
                scores = scores.reshape(STACK, rows, held) + bias[:, :held][None]
                top = jnp.max(scores, axis=2, keepdims=True)
                exponent = jnp.exp2((scores - top) * rate)
                totals = jnp.sum(exponent, axis=2, keepdims=True)
                weights = exponent.astype(jnp.bfloat16).reshape(STACK * rows, held)
                mixed = jnp.dot(weights, values, preferred_element_type=jnp.float32)
                mixed = (mixed.reshape(STACK, rows, HEAD_WIDTH) / totals).astype(jnp.bfloat16)
                for i in range(STACK):
                    o_buf[turn, :, (h + i) * HEAD_WIDTH : (h + i + 1) * HEAD_WIDTH] = mixed[i]
            leaving(g, "start")
            return carry

        lax.fori_loop(0, span, one_group, 0)

    pl.when(reaches)(lambda: attention(5))
    pl.when(jnp.logical_not(reaches))(lambda: attention(3))
    for g in range(max(span - 2, 0), span):
        leaving(g, "wait")
    clearing("wait")


def attend(pick, queries, window, offset, marked, out, first, last):
    rows, width = queries.shape
    span = last - first
    slots = pick.shape[0]
    blocks = 5
    chained = [] if out is None else [out]
    anywhere = pl.BlockSpec(memory_space=pl.ANY)
    return pl.pallas_call(
        functools.partial(attend_kernel, first, span, offset, len(chained)),
        in_specs=[pl.BlockSpec(memory_space=pltpu.SMEM)]
        + [anywhere] * (1 + len(window) + len(marked))
        + [IN_HBM] * len(chained),
        out_specs=[anywhere, IN_HBM],
        out_shape=[
            jax.ShapeDtypeStruct((rows, span * GROUP_COLS), jnp.bfloat16),
            pltpu.HBM((slots * rows, width), jnp.bfloat16),
        ],
        input_output_aliases={2 + len(window) + len(marked): 1} if chained else {},
        scratch_shapes=[
            pltpu.VMEM((2, rows, GROUP_COLS), jnp.bfloat16),
            pltpu.VMEM((2, blocks * rows, 2 * HEAD_WIDTH), jnp.bfloat16),
            pltpu.VMEM((2, rows, GROUP_COLS), jnp.bfloat16),
            pltpu.VMEM((rows, GROUP_COLS), jnp.bfloat16),
            pltpu.VMEM((blocks, rows, MARK_COLS), jnp.bfloat16),
            pltpu.VMEM((rows, blocks * rows), jnp.float32),
            pltpu.SemaphoreType.DMA((2,)),
            pltpu.SemaphoreType.DMA((2, blocks)),
            pltpu.SemaphoreType.DMA((2, slots + 1)),
            pltpu.SemaphoreType.DMA((slots, span)),
            pltpu.SemaphoreType.DMA((blocks,)),
        ],
        compiler_params=pltpu.CompilerParams(vmem_limit_bytes=24 * 1024 * 1024),
        cost_estimate=pl.CostEstimate(flops=0, bytes_accessed=0, transcendentals=0),
    )(pick, queries, *window, *marked, *chained)


def deliver_kernel(starts, pick_ref, *refs):
    got = refs[: len(starts)]
    out_ref, sems = refs[len(starts) + 1 :]
    rows = got[0].shape[0]
    for slot in range(pick_ref.shape[0]):

        @pl.when(pick_ref[slot] == 2)
        def _(slot=slot):
            copies = [
                pltpu.make_async_copy(
                    ref, out_ref.at[pl.ds(slot * rows, rows), pl.ds(c, ref.shape[1])], sems.at[i]
                )
                for i, (ref, c) in enumerate(zip(got, starts))
            ]
            for copy in copies:
                copy.start()
            for copy in copies:
                copy.wait()


def deliver(pick, got, starts, out):
    return pl.pallas_call(
        functools.partial(deliver_kernel, starts),
        grid=(1,),
        in_specs=[pl.BlockSpec(memory_space=pltpu.SMEM)]
        + [pl.BlockSpec(g.shape, lambda i: (0, 0)) for g in got]
        + [IN_HBM],
        out_specs=IN_HBM,
        out_shape=pltpu.HBM(out.shape, out.dtype),
        input_output_aliases={1 + len(got): 0},
        scratch_shapes=[pltpu.SemaphoreType.DMA((len(got),))],
        compiler_params=pltpu.CompilerParams(vmem_limit_bytes=24 * 1024 * 1024),
    )(pick, *got, out)


def local(queries, keyvalue, doc_ids, owner_tiles, tile_counts):
    count = lax.axis_size("seq")
    half = count // 2

    far = [(i, i + 2 * CORES) for i in range(count - 2 * CORES)]
    near = [(i, i + CORES) for i in range(count - CORES)]
    cross = [(i, i ^ 1) for i in range(count)]
    cross_up = [p for p in cross if p[0] % CORES == 0]
    cross_down = [p for p in cross if p[0] % CORES == 1]
    split = SPANS[0][1]
    cut = split * 2 * HEAD_WIDTH
    marked, rest, pick, mode = prepare(keyvalue, doc_ids, owner_tiles, tile_counts, cut)
    far_early, near_early = send(marked, far), send(marked, near)
    far_late, near_late = send(rest, far), send(rest, near)
    own_early, own_late = send(marked, cross_up), send(rest, cross_up)

    def window(far_block, near_block, own_crossed, own):
        return [send(near_block, cross), own_crossed, near_block, send(far_block, cross_down), far_block, own]

    early = window(far_early, near_early, own_early, marked)
    part, out = attend(pick, queries, early, 0, early, None, *SPANS[0])
    part, far_late, near_late = lax.optimization_barrier((part, far_late, near_late))
    late = window(far_late, near_late, own_late, rest)

    up = [(i, i + half) for i in range(half)]
    down = [(i + half, i) for i in range(half)]
    starts = [first * GROUP_COLS for first, _ in SPANS]

    def moving(pairs):
        def branch(pick, queries, part, out, early, late):
            got = []
            for first, last in SPANS[1:]:
                if pairs:
                    got.append(send(part, pairs))
                part, out = attend(pick, queries, late, split, early, out, first, last)
            if pairs:
                got.append(send(part, pairs))
                for part, start in zip(got, starts):
                    out = deliver(pick, [part], [start], out)
            return out

        return branch

    branches = [moving(None), moving(up), moving(down), moving(up + down)]
    return lax.switch(mode[0], branches, pick, queries, part, out, early, late)


def solution(mesh):
    placed = (
        P(("groups", "seq"), None),
        P(("groups", "seq"), None),
        P(("groups", "seq")),
        P(("groups", "seq"), None),
        P(("groups", "seq")),
    )
    return jax.shard_map(
        local, mesh=mesh, in_specs=placed, out_specs=P(("groups", "seq"), None), check_vma=False
    )
```

```python
import functools
import math

import jax
import jax.numpy as jnp
from jax import lax
from jax.experimental import pallas as pl
from jax.experimental.pallas import tpu as pltpu
from jax.sharding import PartitionSpec as P

QUERY_HEADS = 64
KEY_VALUE_HEADS = 8
HEAD_WIDTH = 128
TILE = 128
DOCUMENT_LIMIT = 512
GROUP = QUERY_HEADS // KEY_VALUE_HEADS
GROUP_COLS = GROUP * HEAD_WIDTH
MARK_ROWS = 16
CORES = 2
STACK = 4
SPANS = ((0, 3), (3, 6), (6, 8))
MASKED = -1e30
IN_HBM = pl.BlockSpec(memory_space=pltpu.HBM)


def send(block, pairs):
    return lax.ppermute(block, "seq", pairs)


def stacked_rows(ref, out_ref, first):
    rows, cols = ref.shape
    for c in range(first, cols // HEAD_WIDTH):
        out_ref[(c - first) * rows : (c - first + 1) * rows, :] = ref[:, c * HEAD_WIDTH : (c + 1) * HEAD_WIDTH]


def early_kernel(doc_ref, kv_ref, early_ref):
    stacked_rows(kv_ref, early_ref, 0)
    marks = (doc_ref[...] + 1).astype(jnp.float32)
    early_ref[early_ref.shape[0] - MARK_ROWS :, :] = jnp.broadcast_to(marks, (MARK_ROWS, marks.shape[1])).astype(
        jnp.bfloat16
    )


def prepare_early(keyvalue, doc_ids, cut):
    rows = keyvalue.shape[0]
    shape = (rows * cut // HEAD_WIDTH + MARK_ROWS, HEAD_WIDTH)
    return pl.pallas_call(
        early_kernel,
        grid=(1,),
        in_specs=[pl.BlockSpec((1, rows), lambda i: (0, 0)), pl.BlockSpec((rows, cut), lambda i: (0, 0))],
        out_specs=pl.BlockSpec(shape, lambda i: (0, 0)),
        out_shape=jax.ShapeDtypeStruct(shape, jnp.bfloat16),
    )(doc_ids.reshape(1, rows), keyvalue)


def late_kernel(first, kv_ref, tiles_ref, counts_ref, late_ref, pick_ref, mode_ref):
    stacked_rows(kv_ref, late_ref, first)
    me = lax.axis_index("seq")
    held = counts_ref[0]
    for slot in range(pick_ref.shape[0]):
        kind = jnp.where(tiles_ref[0, slot] == me, 1, 2)
        pick_ref[slot] = jnp.where(slot < held, kind, 0).astype(jnp.int32)
    lower = me < lax.axis_size("seq") // 2
    alone = jnp.where((held == 0) == lower, 1, 2)
    mode_ref[0] = jnp.where(held == 1, jnp.where(tiles_ref[0, 0] == me, 0, 3), alone).astype(jnp.int32)


def prepare_late(keyvalue, owner_tiles, tile_counts, cut):
    rows, cols = keyvalue.shape
    slots = owner_tiles.shape[1]
    scalars = pl.BlockSpec(memory_space=pltpu.SMEM)
    shape = (rows * (cols - cut) // HEAD_WIDTH, HEAD_WIDTH)
    return pl.pallas_call(
        functools.partial(late_kernel, cut // HEAD_WIDTH),
        grid=(1,),
        in_specs=[pl.BlockSpec((rows, cols), lambda i: (0, 0))] + [scalars] * 2,
        out_specs=[pl.BlockSpec(shape, lambda i: (0, 0))] + [scalars] * 2,
        out_shape=[
            jax.ShapeDtypeStruct(shape, jnp.bfloat16),
            jax.ShapeDtypeStruct((slots,), jnp.int32),
            jax.ShapeDtypeStruct((1,), jnp.int32),
        ],
    )(keyvalue, owner_tiles, tile_counts)


def attend_kernel(first, span, offset, chained, pick_ref, q_hbm, *refs):
    kv_refs, mark_refs = refs[:6], refs[6:12]
    scratch = refs[12 + chained :]
    part_ref, out_ref, q_buf, k_buf, v_buf, o_buf, blank, marks, bias = scratch[:9]
    q_sems, k_sems, v_sems, o_sems, blank_sems, mark_sems = scratch[9:]
    rows = q_buf.shape[1]
    slots = pick_ref.shape[0]
    first_core = lax.axis_index("seq") % CORES == 0
    rate = HEAD_WIDTH**-0.5 * math.log2(math.e)
    mark_place = mark_refs[0].shape[0] - MARK_ROWS

    def nearest_first(use):
        use(0, 5)
        pl.when(first_core)(lambda: use(1, 0))
        pl.when(jnp.logical_not(first_core))(lambda: use(1, 1))
        use(2, 2)
        pl.when(first_core)(lambda: use(3, 3))
        pl.when(jnp.logical_not(first_core))(lambda: use(3, 0))
        use(4, 4)

    def cols_of(g, width):
        return pl.ds(pl.multiple_of(g * width, width), width)

    def arriving(g, step):
        turn = lax.rem(g, 2)
        copy = pltpu.make_async_copy(
            q_hbm.at[:, cols_of(first + g, GROUP_COLS)], q_buf.at[turn], q_sems.at[turn]
        )
        getattr(copy, step)()

        def block(b, i):
            copy = pltpu.make_async_copy(
                kv_refs[i].at[cols_of(2 * (first - offset + g), rows), :],
                k_buf.at[turn, pl.ds(b * rows, rows), :],
                k_sems.at[turn, b],
            )
            getattr(copy, step)()
            copy = pltpu.make_async_copy(
                kv_refs[i].at[cols_of(2 * (first - offset + g) + 1, rows), :],
                v_buf.at[turn, pl.ds(b * rows, rows), :],
                v_sems.at[turn, b],
            )
            getattr(copy, step)()

        nearest_first(block)

    def reading_marks(step):
        def block(b, i):
            copy = pltpu.make_async_copy(
                mark_refs[i].at[pl.ds(mark_place, MARK_ROWS), :], marks.at[b], mark_sems.at[b]
            )
            getattr(copy, step)()

        nearest_first(block)

    def leaving(g, step):
        turn = lax.rem(g, 2)
        copy = pltpu.make_async_copy(o_buf.at[turn], part_ref.at[:, cols_of(g, GROUP_COLS)], o_sems.at[turn, slots])
        getattr(copy, step)()
        for slot in range(slots):
            there = out_ref.at[pl.ds(slot * rows, rows), cols_of(first + g, GROUP_COLS)]
            copy = pltpu.make_async_copy(o_buf.at[turn], there, o_sems.at[turn, slot])
            pl.when(pick_ref[slot] == 1)(getattr(copy, step))

    def clearing(step):
        for slot in range(slots):

            @pl.when(pick_ref[slot] == 0)
            def _(slot=slot):
                for g in range(span):
                    there = out_ref.at[pl.ds(slot * rows, rows), pl.ds((first + g) * GROUP_COLS, GROUP_COLS)]
                    getattr(pltpu.make_async_copy(blank, there, blank_sems.at[slot, g]), step)()

    reading_marks("start")
    arriving(0, "start")
    blank[...] = jnp.zeros_like(blank)
    clearing("start")
    reading_marks("wait")
    mine = jnp.broadcast_to(marks[0, 0:1, :].astype(jnp.float32), (rows, rows)).T
    for b in range(marks.shape[0]):
        same = mine == marks[b, 0:1, :].astype(jnp.float32)
        if b == 0:
            q_place = lax.broadcasted_iota(jnp.int32, (rows, rows), 0)
            k_place = lax.broadcasted_iota(jnp.int32, (rows, rows), 1)
            same = same & (k_place <= q_place)
        bias[:, b * rows : (b + 1) * rows] = jnp.where(same, 0.0, MASKED)
    third = marks[3, 0:1, :].astype(jnp.float32)
    reaches = jnp.max(jnp.where(third == marks[0, 0:1, 0:1].astype(jnp.float32), 1.0, 0.0)) > 0.5

    def attention(blocks):
        held = blocks * rows

        def one_group(g, carry):
            turn = lax.rem(g, 2)
            pl.when(g + 1 < span)(lambda: arriving(g + 1, "start"))
            arriving(g, "wait")
            pl.when(g >= 2)(lambda: leaving(g - 2, "wait"))
            keys, values = k_buf[turn, :held, :], v_buf[turn, :held, :]
            for h in range(0, GROUP, STACK):
                q = jnp.concatenate(
                    [q_buf[turn, :, (h + i) * HEAD_WIDTH : (h + i + 1) * HEAD_WIDTH] for i in range(STACK)], axis=0
                )
                scores = lax.dot_general(q, keys, (((1,), (1,)), ((), ())), preferred_element_type=jnp.float32)
                scores = scores.reshape(STACK, rows, held) + bias[:, :held][None]
                top = jnp.max(scores, axis=2, keepdims=True)
                exponent = jnp.exp2((scores - top) * rate)
                totals = jnp.sum(exponent, axis=2, keepdims=True)
                weights = exponent.astype(jnp.bfloat16).reshape(STACK * rows, held)
                mixed = jnp.dot(weights, values, preferred_element_type=jnp.float32)
                mixed = (mixed.reshape(STACK, rows, HEAD_WIDTH) / totals).astype(jnp.bfloat16)
                for i in range(STACK):
                    o_buf[turn, :, (h + i) * HEAD_WIDTH : (h + i + 1) * HEAD_WIDTH] = mixed[i]
            leaving(g, "start")
            return carry

        lax.fori_loop(0, span, one_group, 0)

    pl.when(reaches)(lambda: attention(5))
    pl.when(jnp.logical_not(reaches))(lambda: attention(3))
    for g in range(max(span - 2, 0), span):
        leaving(g, "wait")
    clearing("wait")


def attend(pick, queries, window, offset, marked, out, first, last):
    rows, width = queries.shape
    span = last - first
    slots = pick.shape[0]
    blocks = 5
    chained = [] if out is None else [out]
    anywhere = pl.BlockSpec(memory_space=pl.ANY)
    return pl.pallas_call(
        functools.partial(attend_kernel, first, span, offset, len(chained)),
        in_specs=[pl.BlockSpec(memory_space=pltpu.SMEM)]
        + [anywhere] * (1 + len(window) + len(marked))
        + [IN_HBM] * len(chained),
        out_specs=[anywhere, IN_HBM],
        out_shape=[
            jax.ShapeDtypeStruct((rows, span * GROUP_COLS), jnp.bfloat16),
            pltpu.HBM((slots * rows, width), jnp.bfloat16),
        ],
        input_output_aliases={2 + len(window) + len(marked): 1} if chained else {},
        scratch_shapes=[
            pltpu.VMEM((2, rows, GROUP_COLS), jnp.bfloat16),
            pltpu.VMEM((2, blocks * rows, HEAD_WIDTH), jnp.bfloat16),
            pltpu.VMEM((2, blocks * rows, HEAD_WIDTH), jnp.bfloat16),
            pltpu.VMEM((2, rows, GROUP_COLS), jnp.bfloat16),
            pltpu.VMEM((rows, GROUP_COLS), jnp.bfloat16),
            pltpu.VMEM((blocks, MARK_ROWS, HEAD_WIDTH), jnp.bfloat16),
            pltpu.VMEM((rows, blocks * rows), jnp.float32),
            pltpu.SemaphoreType.DMA((2,)),
            pltpu.SemaphoreType.DMA((2, blocks)),
            pltpu.SemaphoreType.DMA((2, blocks)),
            pltpu.SemaphoreType.DMA((2, slots + 1)),
            pltpu.SemaphoreType.DMA((slots, span)),
            pltpu.SemaphoreType.DMA((blocks,)),
        ],
        compiler_params=pltpu.CompilerParams(vmem_limit_bytes=24 * 1024 * 1024),
        cost_estimate=pl.CostEstimate(flops=0, bytes_accessed=0, transcendentals=0),
    )(pick, queries, *window, *marked, *chained)


def deliver_kernel(starts, pick_ref, *refs):
    got = refs[: len(starts)]
    out_ref, sems = refs[len(starts) + 1 :]
    rows = got[0].shape[0]
    for slot in range(pick_ref.shape[0]):

        @pl.when(pick_ref[slot] == 2)
        def _(slot=slot):
            copies = [
                pltpu.make_async_copy(
                    ref, out_ref.at[pl.ds(slot * rows, rows), pl.ds(c, ref.shape[1])], sems.at[i]
                )
                for i, (ref, c) in enumerate(zip(got, starts))
            ]
            for copy in copies:
                copy.start()
            for copy in copies:
                copy.wait()


def deliver(pick, got, starts, out):
    return pl.pallas_call(
        functools.partial(deliver_kernel, starts),
        grid=(1,),
        in_specs=[pl.BlockSpec(memory_space=pltpu.SMEM)]
        + [pl.BlockSpec(g.shape, lambda i: (0, 0)) for g in got]
        + [IN_HBM],
        out_specs=IN_HBM,
        out_shape=pltpu.HBM(out.shape, out.dtype),
        input_output_aliases={1 + len(got): 0},
        scratch_shapes=[pltpu.SemaphoreType.DMA((len(got),))],
        compiler_params=pltpu.CompilerParams(vmem_limit_bytes=24 * 1024 * 1024),
    )(pick, *got, out)


def local(queries, keyvalue, doc_ids, owner_tiles, tile_counts):
    count = lax.axis_size("seq")
    half = count // 2

    far = [(i, i + 2 * CORES) for i in range(count - 2 * CORES)]
    near = [(i, i + CORES) for i in range(count - CORES)]
    cross = [(i, i ^ 1) for i in range(count)]
    cross_up = [p for p in cross if p[0] % CORES == 0]
    cross_down = [p for p in cross if p[0] % CORES == 1]
    split = SPANS[0][1]
    cut = split * 2 * HEAD_WIDTH
    marked = prepare_early(keyvalue, doc_ids, cut)
    rest, pick, mode = prepare_late(keyvalue, owner_tiles, tile_counts, cut)
    far_early, near_early = send(marked, far), send(marked, near)
    far_late, near_late = send(rest, far), send(rest, near)
    own_early, own_late = send(marked, cross_up), send(rest, cross_up)

    def window(far_block, near_block, own_crossed, own):
        return [send(near_block, cross), own_crossed, near_block, send(far_block, cross_down), far_block, own]

    early = window(far_early, near_early, own_early, marked)
    part, out = attend(pick, queries, early, 0, early, None, *SPANS[0])
    part, far_late, near_late = lax.optimization_barrier((part, far_late, near_late))
    late = window(far_late, near_late, own_late, rest)

    up = [(i, i + half) for i in range(half)]
    down = [(i + half, i) for i in range(half)]
    starts = [first * GROUP_COLS for first, _ in SPANS]

    def moving(pairs):
        def branch(pick, queries, part, out, early, late):
            got = []
            for first, last in SPANS[1:]:
                if pairs:
                    got.append(send(part, pairs))
                part, out = attend(pick, queries, late, split, early, out, first, last)
            if pairs:
                got.append(send(part, pairs))
                for part, start in zip(got, starts):
                    out = deliver(pick, [part], [start], out)
            return out

        return branch

    branches = [moving(None), moving(up), moving(down), moving(up + down)]
    return lax.switch(mode[0], branches, pick, queries, part, out, early, late)


def solution(mesh):
    placed = (
        P(("groups", "seq"), None),
        P(("groups", "seq"), None),
        P(("groups", "seq")),
        P(("groups", "seq"), None),
        P(("groups", "seq")),
    )
    return jax.shard_map(
        local, mesh=mesh, in_specs=placed, out_specs=P(("groups", "seq"), None), check_vma=False
    )
```

```python
import functools
import math

import jax
import jax.numpy as jnp
from jax import lax
from jax.experimental import pallas as pl
from jax.experimental.pallas import tpu as pltpu
from jax.sharding import PartitionSpec as P

QUERY_HEADS = 64
KEY_VALUE_HEADS = 8
HEAD_WIDTH = 128
TILE = 128
DOCUMENT_LIMIT = 512
GROUP = QUERY_HEADS // KEY_VALUE_HEADS
GROUP_COLS = GROUP * HEAD_WIDTH
MARK_ROWS = 16
NEAR_BLOCKS = 3
CORES = 2
STACK = 8
SPANS = ((0, 3), (3, 6), (6, 8))
MASKED = -1e30
IN_HBM = pl.BlockSpec(memory_space=pltpu.HBM)


def send(block, pairs):
    return lax.ppermute(block, "seq", pairs)


def stacked_rows(ref, out_ref, first):
    rows, cols = ref.shape
    for c in range(first, cols // HEAD_WIDTH):
        out_ref[(c - first) * rows : (c - first + 1) * rows, :] = ref[:, c * HEAD_WIDTH : (c + 1) * HEAD_WIDTH]


def early_kernel(doc_ref, kv_ref, early_ref):
    stacked_rows(kv_ref, early_ref, 0)
    marks = (doc_ref[...] + 1).astype(jnp.float32)
    early_ref[early_ref.shape[0] - MARK_ROWS :, :] = jnp.broadcast_to(marks, (MARK_ROWS, marks.shape[1])).astype(
        jnp.bfloat16
    )


def prepare_early(keyvalue, doc_ids, cut):
    rows = keyvalue.shape[0]
    shape = (rows * cut // HEAD_WIDTH + MARK_ROWS, HEAD_WIDTH)
    return pl.pallas_call(
        early_kernel,
        grid=(1,),
        in_specs=[pl.BlockSpec((1, rows), lambda i: (0, 0)), pl.BlockSpec((rows, cut), lambda i: (0, 0))],
        out_specs=pl.BlockSpec(shape, lambda i: (0, 0)),
        out_shape=jax.ShapeDtypeStruct(shape, jnp.bfloat16),
    )(doc_ids.reshape(1, rows), keyvalue)


def late_kernel(first, kv_ref, tiles_ref, counts_ref, late_ref, pick_ref, mode_ref):
    stacked_rows(kv_ref, late_ref, first)
    me = lax.axis_index("seq")
    held = counts_ref[0]
    for slot in range(pick_ref.shape[0]):
        kind = jnp.where(tiles_ref[0, slot] == me, 1, 2)
        pick_ref[slot] = jnp.where(slot < held, kind, 0).astype(jnp.int32)
    lower = me < lax.axis_size("seq") // 2
    alone = jnp.where((held == 0) == lower, 1, 2)
    mode_ref[0] = jnp.where(held == 1, jnp.where(tiles_ref[0, 0] == me, 0, 3), alone).astype(jnp.int32)


def prepare_late(keyvalue, owner_tiles, tile_counts, cut):
    rows, cols = keyvalue.shape
    slots = owner_tiles.shape[1]
    scalars = pl.BlockSpec(memory_space=pltpu.SMEM)
    shape = (rows * (cols - cut) // HEAD_WIDTH, HEAD_WIDTH)
    return pl.pallas_call(
        functools.partial(late_kernel, cut // HEAD_WIDTH),
        grid=(1,),
        in_specs=[pl.BlockSpec((rows, cols), lambda i: (0, 0))] + [scalars] * 2,
        out_specs=[pl.BlockSpec(shape, lambda i: (0, 0))] + [scalars] * 2,
        out_shape=[
            jax.ShapeDtypeStruct(shape, jnp.bfloat16),
            jax.ShapeDtypeStruct((slots,), jnp.int32),
            jax.ShapeDtypeStruct((1,), jnp.int32),
        ],
    )(keyvalue, owner_tiles, tile_counts)


def attend_kernel(first, span, offset, chained, pick_ref, q_hbm, *refs):
    kv_refs, mark_refs = refs[:6], refs[6:12]
    scratch = refs[12 + chained :]
    part_ref, out_ref, q_buf, kv_buf, o_buf, blank, marks, bias = scratch[:8]
    q_sems, kv_sems, o_sems, blank_sems, mark_sems = scratch[8:]
    rows = q_buf.shape[1]
    slots = pick_ref.shape[0]
    first_core = lax.axis_index("seq") % CORES == 0
    rate = HEAD_WIDTH**-0.5 * math.log2(math.e)
    mark_place = mark_refs[0].shape[0] - MARK_ROWS

    def by_distance(use, first, last):
        for b, by_core in enumerate(((5, 5), (0, 1), (2, 2), (3, 0), (4, 4))[first:last], first):
            if by_core[0] == by_core[1]:
                use(b, by_core[0])
            else:
                pl.when(first_core)(functools.partial(use, b, by_core[0]))
                pl.when(jnp.logical_not(first_core))(functools.partial(use, b, by_core[1]))

    def cols_of(g, width):
        return pl.ds(pl.multiple_of(g * width, width), width)

    def arriving_queries(g, step):
        turn = lax.rem(g, 2)
        copy = pltpu.make_async_copy(
            q_hbm.at[:, cols_of(first + g, GROUP_COLS)], q_buf.at[turn], q_sems.at[turn]
        )
        getattr(copy, step)()

    def arriving_blocks(g, step, begin, end):
        turn = lax.rem(g, 2)

        def block(b, i):
            there = kv_refs[i].at[cols_of(first - offset + g, 2 * rows), :]
            getattr(pltpu.make_async_copy(there, kv_buf.at[turn, b], kv_sems.at[turn, b]), step)()

        by_distance(block, begin, end)

    def reading_marks(step):
        def block(b, i):
            there = mark_refs[i].at[pl.ds(mark_place, MARK_ROWS), :]
            getattr(pltpu.make_async_copy(there, marks.at[b], mark_sems.at[b]), step)()

        by_distance(block, 0, marks.shape[0])

    keeps = functools.reduce(jnp.logical_or, [pick_ref[slot] == 1 for slot in range(slots)])

    def leaving(g, step):
        turn = lax.rem(g, 2)

        @pl.when(jnp.logical_not(keeps))
        def _():
            there = part_ref.at[:, cols_of(g, GROUP_COLS)]
            getattr(pltpu.make_async_copy(o_buf.at[turn], there, o_sems.at[turn, slots]), step)()

        for slot in range(slots):
            there = out_ref.at[pl.ds(slot * rows, rows), cols_of(first + g, GROUP_COLS)]
            copy = pltpu.make_async_copy(o_buf.at[turn], there, o_sems.at[turn, slot])
            pl.when(pick_ref[slot] == 1)(getattr(copy, step))

    def clearing(step):
        for slot in range(slots):

            @pl.when(pick_ref[slot] == 0)
            def _(slot=slot):
                for g in range(span):
                    there = out_ref.at[pl.ds(slot * rows, rows), pl.ds((first + g) * GROUP_COLS, GROUP_COLS)]
                    getattr(pltpu.make_async_copy(blank, there, blank_sems.at[slot, g]), step)()

    reading_marks("start")
    arriving_queries(0, "start")
    arriving_blocks(0, "start", 0, NEAR_BLOCKS)
    blank[...] = jnp.zeros_like(blank)
    clearing("start")
    reading_marks("wait")
    third = marks[NEAR_BLOCKS, 0:1, :].astype(jnp.float32)
    reaches = jnp.max(jnp.where(third == marks[0, 0:1, 0:1].astype(jnp.float32), 1.0, 0.0)) > 0.5
    pl.when(reaches)(lambda: arriving_blocks(0, "start", NEAR_BLOCKS, marks.shape[0]))
    mine = jnp.broadcast_to(marks[0, 0:1, :].astype(jnp.float32), (rows, rows)).T
    for b in range(marks.shape[0]):
        same = mine == marks[b, 0:1, :].astype(jnp.float32)
        if b == 0:
            q_place = lax.broadcasted_iota(jnp.int32, (rows, rows), 0)
            k_place = lax.broadcasted_iota(jnp.int32, (rows, rows), 1)
            same = same & (k_place <= q_place)
        bias[:, b * rows : (b + 1) * rows] = jnp.where(same, 0.0, MASKED)

    def attention(blocks):
        held = blocks * rows

        def one_group(g, carry):
            turn = lax.rem(g, 2)

            @pl.when(g + 1 < span)
            def _():
                arriving_queries(g + 1, "start")
                arriving_blocks(g + 1, "start", 0, blocks)

            arriving_queries(g, "wait")
            arriving_blocks(g, "wait", 0, blocks)
            pl.when(g >= 2)(lambda: leaving(g - 2, "wait"))
            keys = kv_buf[turn, :blocks, :rows, :].reshape(held, HEAD_WIDTH)
            values = kv_buf[turn, :blocks, rows:, :].reshape(held, HEAD_WIDTH)
            for h in range(0, GROUP, STACK):
                q = jnp.concatenate(
                    [q_buf[turn, :, (h + i) * HEAD_WIDTH : (h + i + 1) * HEAD_WIDTH] for i in range(STACK)], axis=0
                )
                scores = lax.dot_general(q, keys, (((1,), (1,)), ((), ())), preferred_element_type=jnp.float32)
                scores = scores.reshape(STACK, rows, held) + bias[:, :held][None]
                top = jnp.max(scores, axis=2, keepdims=True)
                exponent = jnp.exp2((scores - top) * rate)
                totals = jnp.sum(exponent, axis=2, keepdims=True)
                weights = exponent.astype(jnp.bfloat16).reshape(STACK * rows, held)
                mixed = jnp.dot(weights, values, preferred_element_type=jnp.float32)
                mixed = (mixed.reshape(STACK, rows, HEAD_WIDTH) / totals).astype(jnp.bfloat16)
                for i in range(STACK):
                    o_buf[turn, :, (h + i) * HEAD_WIDTH : (h + i + 1) * HEAD_WIDTH] = mixed[i]
            leaving(g, "start")
            return carry

        lax.fori_loop(0, span, one_group, 0)

    pl.when(reaches)(lambda: attention(marks.shape[0]))
    pl.when(jnp.logical_not(reaches))(lambda: attention(NEAR_BLOCKS))
    for g in range(max(span - 2, 0), span):
        leaving(g, "wait")
    clearing("wait")


def attend(pick, queries, window, offset, marked, out, first, last):
    rows, width = queries.shape
    span = last - first
    slots = pick.shape[0]
    blocks = 5
    chained = [] if out is None else [out]
    anywhere = pl.BlockSpec(memory_space=pl.ANY)
    return pl.pallas_call(
        functools.partial(attend_kernel, first, span, offset, len(chained)),
        in_specs=[pl.BlockSpec(memory_space=pltpu.SMEM)]
        + [anywhere] * (1 + len(window) + len(marked))
        + [IN_HBM] * len(chained),
        out_specs=[anywhere, IN_HBM],
        out_shape=[
            jax.ShapeDtypeStruct((rows, span * GROUP_COLS), jnp.bfloat16),
            pltpu.HBM((slots * rows, width), jnp.bfloat16),
        ],
        input_output_aliases={2 + len(window) + len(marked): 1} if chained else {},
        scratch_shapes=[
            pltpu.VMEM((2, rows, GROUP_COLS), jnp.bfloat16),
            pltpu.VMEM((2, blocks, 2 * rows, HEAD_WIDTH), jnp.bfloat16),
            pltpu.VMEM((2, rows, GROUP_COLS), jnp.bfloat16),
            pltpu.VMEM((rows, GROUP_COLS), jnp.bfloat16),
            pltpu.VMEM((blocks, MARK_ROWS, HEAD_WIDTH), jnp.bfloat16),
            pltpu.VMEM((rows, blocks * rows), jnp.float32),
            pltpu.SemaphoreType.DMA((2,)),
            pltpu.SemaphoreType.DMA((2, blocks)),
            pltpu.SemaphoreType.DMA((2, slots + 1)),
            pltpu.SemaphoreType.DMA((slots, span)),
            pltpu.SemaphoreType.DMA((blocks,)),
        ],
        compiler_params=pltpu.CompilerParams(vmem_limit_bytes=24 * 1024 * 1024),
        cost_estimate=pl.CostEstimate(flops=0, bytes_accessed=0, transcendentals=0),
    )(pick, queries, *window, *marked, *chained)


def deliver_kernel(starts, pick_ref, *refs):
    got = refs[: len(starts)]
    out_ref, sems = refs[len(starts) + 1 :]
    rows = got[0].shape[0]
    for slot in range(pick_ref.shape[0]):

        @pl.when(pick_ref[slot] == 2)
        def _(slot=slot):
            copies = [
                pltpu.make_async_copy(
                    ref, out_ref.at[pl.ds(slot * rows, rows), pl.ds(c, ref.shape[1])], sems.at[i]
                )
                for i, (ref, c) in enumerate(zip(got, starts))
            ]
            for copy in copies:
                copy.start()
            for copy in copies:
                copy.wait()


def deliver(pick, got, starts, out):
    return pl.pallas_call(
        functools.partial(deliver_kernel, starts),
        grid=(1,),
        in_specs=[pl.BlockSpec(memory_space=pltpu.SMEM)]
        + [pl.BlockSpec(g.shape, lambda i: (0, 0)) for g in got]
        + [IN_HBM],
        out_specs=IN_HBM,
        out_shape=pltpu.HBM(out.shape, out.dtype),
        input_output_aliases={1 + len(got): 0},
        scratch_shapes=[pltpu.SemaphoreType.DMA((len(got),))],
        compiler_params=pltpu.CompilerParams(vmem_limit_bytes=24 * 1024 * 1024),
    )(pick, *got, out)


def local(queries, keyvalue, doc_ids, owner_tiles, tile_counts):
    count = lax.axis_size("seq")
    half = count // 2

    far = [(i, i + 2 * CORES) for i in range(count - 2 * CORES)]
    near = [(i, i + CORES) for i in range(count - CORES)]
    cross = [(i, i ^ 1) for i in range(count)]
    cross_up = [p for p in cross if p[0] % CORES == 0]
    cross_down = [p for p in cross if p[0] % CORES == 1]
    split = SPANS[0][1]
    cut = split * 2 * HEAD_WIDTH
    marked = prepare_early(keyvalue, doc_ids, cut)
    rest, pick, mode = prepare_late(keyvalue, owner_tiles, tile_counts, cut)
    far_early, near_early = send(marked, far), send(marked, near)
    far_late, near_late = send(rest, far), send(rest, near)
    own_early, own_late = send(marked, cross_up), send(rest, cross_up)

    def window(far_block, near_block, own_crossed, own):
        return [send(near_block, cross), own_crossed, near_block, send(far_block, cross_down), far_block, own]

    early = window(far_early, near_early, own_early, marked)
    part, out = attend(pick, queries, early, 0, early, None, *SPANS[0])
    part, far_late, near_late = lax.optimization_barrier((part, far_late, near_late))
    late = window(far_late, near_late, own_late, rest)

    up = [(i, i + half) for i in range(half)]
    down = [(i + half, i) for i in range(half)]
    starts = [first * GROUP_COLS for first, _ in SPANS]

    def moving(pairs):
        def branch(pick, queries, part, out, early, late):
            got = []
            for first, last in SPANS[1:]:
                if pairs:
                    got.append(send(part, pairs))
                part, out = attend(pick, queries, late, split, early, out, first, last)
            if pairs:
                got.append(send(part, pairs))
                for part, start in zip(got, starts):
                    out = deliver(pick, [part], [start], out)
            return out

        return branch

    branches = [moving(None), moving(up), moving(down), moving(up + down)]
    return lax.switch(mode[0], branches, pick, queries, part, out, early, late)


def solution(mesh):
    placed = (
        P(("groups", "seq"), None),
        P(("groups", "seq"), None),
        P(("groups", "seq")),
        P(("groups", "seq"), None),
        P(("groups", "seq")),
    )
    return jax.shard_map(
        local, mesh=mesh, in_specs=placed, out_specs=P(("groups", "seq"), None), check_vma=False
    )
```

```python
import functools
import math

import jax
import jax.numpy as jnp
from jax import lax
from jax.experimental import pallas as pl
from jax.experimental.pallas import tpu as pltpu
from jax.sharding import PartitionSpec as P

QUERY_HEADS = 64
KEY_VALUE_HEADS = 8
HEAD_WIDTH = 128
TILE = 128
DOCUMENT_LIMIT = 512
GROUP = QUERY_HEADS // KEY_VALUE_HEADS
GROUP_COLS = GROUP * HEAD_WIDTH
MARK_ROWS = 16
NEAR_BLOCKS = 3
CORES = 2
STACK = 8
SPANS = ((0, 3), (3, 6), (6, 8))
MASKED = -1e30
IN_HBM = pl.BlockSpec(memory_space=pltpu.HBM)


def send(block, pairs):
    return lax.ppermute(block, "seq", pairs)


def stacked_rows(ref, out_ref, first):
    rows, cols = ref.shape
    for c in range(first, cols // HEAD_WIDTH):
        out_ref[(c - first) * rows : (c - first + 1) * rows, :] = ref[:, c * HEAD_WIDTH : (c + 1) * HEAD_WIDTH]


def early_kernel(doc_ref, kv_ref, early_ref):
    stacked_rows(kv_ref, early_ref, 0)
    marks = (doc_ref[...] + 1).astype(jnp.float32)
    early_ref[early_ref.shape[0] - MARK_ROWS :, :] = jnp.broadcast_to(marks, (MARK_ROWS, marks.shape[1])).astype(
        jnp.bfloat16
    )


def prepare_early(keyvalue, doc_ids, cut):
    rows = keyvalue.shape[0]
    shape = (rows * cut // HEAD_WIDTH + MARK_ROWS, HEAD_WIDTH)
    return pl.pallas_call(
        early_kernel,
        grid=(1,),
        in_specs=[pl.BlockSpec((1, rows), lambda i: (0, 0)), pl.BlockSpec((rows, cut), lambda i: (0, 0))],
        out_specs=pl.BlockSpec(shape, lambda i: (0, 0)),
        out_shape=jax.ShapeDtypeStruct(shape, jnp.bfloat16),
    )(doc_ids.reshape(1, rows), keyvalue)


def late_kernel(first, kv_ref, tiles_ref, counts_ref, late_ref, pick_ref, mode_ref):
    stacked_rows(kv_ref, late_ref, first)
    me = lax.axis_index("seq")
    held = counts_ref[0]
    for slot in range(pick_ref.shape[0]):
        kind = jnp.where(tiles_ref[0, slot] == me, 1, 2)
        pick_ref[slot] = jnp.where(slot < held, kind, 0).astype(jnp.int32)
    lower = me < lax.axis_size("seq") // 2
    alone = jnp.where((held == 0) == lower, 1, 2)
    mode_ref[0] = jnp.where(held == 1, jnp.where(tiles_ref[0, 0] == me, 0, 3), alone).astype(jnp.int32)


def prepare_late(keyvalue, owner_tiles, tile_counts, cut):
    rows, cols = keyvalue.shape
    slots = owner_tiles.shape[1]
    scalars = pl.BlockSpec(memory_space=pltpu.SMEM)
    shape = (rows * (cols - cut) // HEAD_WIDTH, HEAD_WIDTH)
    return pl.pallas_call(
        functools.partial(late_kernel, cut // HEAD_WIDTH),
        grid=(1,),
        in_specs=[pl.BlockSpec((rows, cols), lambda i: (0, 0))] + [scalars] * 2,
        out_specs=[pl.BlockSpec(shape, lambda i: (0, 0))] + [scalars] * 2,
        out_shape=[
            jax.ShapeDtypeStruct(shape, jnp.bfloat16),
            jax.ShapeDtypeStruct((slots,), jnp.int32),
            jax.ShapeDtypeStruct((1,), jnp.int32),
        ],
    )(keyvalue, owner_tiles, tile_counts)


def attend_kernel(first, span, offset, chained, pick_ref, q_hbm, *refs):
    kv_refs, mark_refs = refs[:6], refs[6:12]
    scratch = refs[12 + chained :]
    part_ref, out_ref, q_buf, kv_buf, o_buf, blank, marks, bias = scratch[:8]
    q_sems, kv_sems, o_sems, blank_sems, mark_sems = scratch[8:]
    rows = q_buf.shape[1]
    slots = pick_ref.shape[0]
    first_core = lax.axis_index("seq") % CORES == 0
    rate = HEAD_WIDTH**-0.5 * math.log2(math.e)
    mark_place = mark_refs[0].shape[0] - MARK_ROWS

    def by_distance(use, first, last):
        for b, by_core in enumerate(((5, 5), (0, 1), (2, 2), (3, 0), (4, 4))[first:last], first):
            if by_core[0] == by_core[1]:
                use(b, by_core[0])
            else:
                pl.when(first_core)(functools.partial(use, b, by_core[0]))
                pl.when(jnp.logical_not(first_core))(functools.partial(use, b, by_core[1]))

    def cols_of(g, width):
        return pl.ds(pl.multiple_of(g * width, width), width)

    def arriving_queries(g, step):
        turn = lax.rem(g, 2)
        copy = pltpu.make_async_copy(
            q_hbm.at[:, cols_of(first + g, GROUP_COLS)], q_buf.at[turn], q_sems.at[turn]
        )
        getattr(copy, step)()

    def arriving_blocks(g, step, begin, end):
        turn = lax.rem(g, 2)

        def block(b, i):
            base = kv_refs[5].shape[0] if i in (1, 3) and kv_refs[i].shape[0] > kv_refs[5].shape[0] else 0
            start = pl.multiple_of(base + (first - offset + g) * 2 * rows, MARK_ROWS)
            there = kv_refs[i].at[pl.ds(start, 2 * rows), :]
            getattr(pltpu.make_async_copy(there, kv_buf.at[turn, b], kv_sems.at[turn, b]), step)()

        by_distance(block, begin, end)

    def reading_marks(step):
        def block(b, i):
            there = mark_refs[i].at[pl.ds(mark_place, MARK_ROWS), :]
            getattr(pltpu.make_async_copy(there, marks.at[b], mark_sems.at[b]), step)()

        by_distance(block, 0, marks.shape[0])

    keeps = functools.reduce(jnp.logical_or, [pick_ref[slot] == 1 for slot in range(slots)])

    def leaving(g, step):
        turn = lax.rem(g, 2)

        @pl.when(jnp.logical_not(keeps))
        def _():
            there = part_ref.at[:, cols_of(g, GROUP_COLS)]
            getattr(pltpu.make_async_copy(o_buf.at[turn], there, o_sems.at[turn, slots]), step)()

        for slot in range(slots):
            there = out_ref.at[pl.ds(slot * rows, rows), cols_of(first + g, GROUP_COLS)]
            copy = pltpu.make_async_copy(o_buf.at[turn], there, o_sems.at[turn, slot])
            pl.when(pick_ref[slot] == 1)(getattr(copy, step))

    def clearing(step):
        for slot in range(slots):

            @pl.when(pick_ref[slot] == 0)
            def _(slot=slot):
                for g in range(span):
                    there = out_ref.at[pl.ds(slot * rows, rows), pl.ds((first + g) * GROUP_COLS, GROUP_COLS)]
                    getattr(pltpu.make_async_copy(blank, there, blank_sems.at[slot, g]), step)()

    reading_marks("start")
    arriving_queries(0, "start")
    arriving_blocks(0, "start", 0, NEAR_BLOCKS)
    blank[...] = jnp.zeros_like(blank)
    clearing("start")
    reading_marks("wait")
    third = marks[NEAR_BLOCKS, 0:1, :].astype(jnp.float32)
    reaches = jnp.max(jnp.where(third == marks[0, 0:1, 0:1].astype(jnp.float32), 1.0, 0.0)) > 0.5
    pl.when(reaches)(lambda: arriving_blocks(0, "start", NEAR_BLOCKS, marks.shape[0]))
    mine = jnp.broadcast_to(marks[0, 0:1, :].astype(jnp.float32), (rows, rows)).T
    for b in range(marks.shape[0]):
        same = mine == marks[b, 0:1, :].astype(jnp.float32)
        if b == 0:
            q_place = lax.broadcasted_iota(jnp.int32, (rows, rows), 0)
            k_place = lax.broadcasted_iota(jnp.int32, (rows, rows), 1)
            same = same & (k_place <= q_place)
        bias[:, b * rows : (b + 1) * rows] = jnp.where(same, 0.0, MASKED)

    def attention(blocks):
        held = blocks * rows

        def one_group(g, carry):
            turn = lax.rem(g, 2)

            @pl.when(g + 1 < span)
            def _():
                arriving_queries(g + 1, "start")
                arriving_blocks(g + 1, "start", 0, blocks)

            arriving_queries(g, "wait")
            arriving_blocks(g, "wait", 0, blocks)
            pl.when(g >= 2)(lambda: leaving(g - 2, "wait"))
            keys = kv_buf[turn, :blocks, :rows, :].reshape(held, HEAD_WIDTH)
            values = kv_buf[turn, :blocks, rows:, :].reshape(held, HEAD_WIDTH)
            for h in range(0, GROUP, STACK):
                q = jnp.concatenate(
                    [q_buf[turn, :, (h + i) * HEAD_WIDTH : (h + i + 1) * HEAD_WIDTH] for i in range(STACK)], axis=0
                )
                scores = lax.dot_general(q, keys, (((1,), (1,)), ((), ())), preferred_element_type=jnp.float32)
                scores = scores.reshape(STACK, rows, held) + bias[:, :held][None]
                top = jnp.max(scores, axis=2, keepdims=True)
                exponent = jnp.exp2((scores - top) * rate)
                totals = jnp.sum(exponent, axis=2, keepdims=True)
                weights = exponent.astype(jnp.bfloat16).reshape(STACK * rows, held)
                mixed = jnp.dot(weights, values, preferred_element_type=jnp.float32)
                mixed = (mixed.reshape(STACK, rows, HEAD_WIDTH) / totals).astype(jnp.bfloat16)
                for i in range(STACK):
                    o_buf[turn, :, (h + i) * HEAD_WIDTH : (h + i + 1) * HEAD_WIDTH] = mixed[i]
            leaving(g, "start")
            return carry

        lax.fori_loop(0, span, one_group, 0)

    pl.when(reaches)(lambda: attention(marks.shape[0]))
    pl.when(jnp.logical_not(reaches))(lambda: attention(NEAR_BLOCKS))
    for g in range(max(span - 2, 0), span):
        leaving(g, "wait")
    clearing("wait")


def attend(pick, queries, window, offset, marked, out, first, last):
    rows, width = queries.shape
    span = last - first
    slots = pick.shape[0]
    blocks = 5
    chained = [] if out is None else [out]
    anywhere = pl.BlockSpec(memory_space=pl.ANY)
    return pl.pallas_call(
        functools.partial(attend_kernel, first, span, offset, len(chained)),
        in_specs=[pl.BlockSpec(memory_space=pltpu.SMEM)]
        + [anywhere] * (1 + len(window) + len(marked))
        + [IN_HBM] * len(chained),
        out_specs=[anywhere, IN_HBM],
        out_shape=[
            jax.ShapeDtypeStruct((rows, span * GROUP_COLS), jnp.bfloat16),
            pltpu.HBM((slots * rows, width), jnp.bfloat16),
        ],
        input_output_aliases={2 + len(window) + len(marked): 1} if chained else {},
        scratch_shapes=[
            pltpu.VMEM((2, rows, GROUP_COLS), jnp.bfloat16),
            pltpu.VMEM((2, blocks, 2 * rows, HEAD_WIDTH), jnp.bfloat16),
            pltpu.VMEM((2, rows, GROUP_COLS), jnp.bfloat16),
            pltpu.VMEM((rows, GROUP_COLS), jnp.bfloat16),
            pltpu.VMEM((blocks, MARK_ROWS, HEAD_WIDTH), jnp.bfloat16),
            pltpu.VMEM((rows, blocks * rows), jnp.float32),
            pltpu.SemaphoreType.DMA((2,)),
            pltpu.SemaphoreType.DMA((2, blocks)),
            pltpu.SemaphoreType.DMA((2, slots + 1)),
            pltpu.SemaphoreType.DMA((slots, span)),
            pltpu.SemaphoreType.DMA((blocks,)),
        ],
        compiler_params=pltpu.CompilerParams(vmem_limit_bytes=24 * 1024 * 1024),
        cost_estimate=pl.CostEstimate(flops=0, bytes_accessed=0, transcendentals=0),
    )(pick, queries, *window, *marked, *chained)


def deliver_kernel(starts, pick_ref, *refs):
    got = refs[: len(starts)]
    out_ref, sems = refs[len(starts) + 1 :]
    rows = got[0].shape[0]
    for slot in range(pick_ref.shape[0]):

        @pl.when(pick_ref[slot] == 2)
        def _(slot=slot):
            copies = [
                pltpu.make_async_copy(
                    ref, out_ref.at[pl.ds(slot * rows, rows), pl.ds(c, ref.shape[1])], sems.at[i]
                )
                for i, (ref, c) in enumerate(zip(got, starts))
            ]
            for copy in copies:
                copy.start()
            for copy in copies:
                copy.wait()


def deliver(pick, got, starts, out):
    return pl.pallas_call(
        functools.partial(deliver_kernel, starts),
        grid=(1,),
        in_specs=[pl.BlockSpec(memory_space=pltpu.SMEM)]
        + [pl.BlockSpec(g.shape, lambda i: (0, 0)) for g in got]
        + [IN_HBM],
        out_specs=IN_HBM,
        out_shape=pltpu.HBM(out.shape, out.dtype),
        input_output_aliases={1 + len(got): 0},
        scratch_shapes=[pltpu.SemaphoreType.DMA((len(got),))],
        compiler_params=pltpu.CompilerParams(vmem_limit_bytes=24 * 1024 * 1024),
    )(pick, *got, out)


def local(queries, keyvalue, doc_ids, owner_tiles, tile_counts):
    count = lax.axis_size("seq")
    half = count // 2

    far = [(i, i + 2 * CORES) for i in range(count - 2 * CORES)]
    near = [(i, i + CORES) for i in range(count - CORES)]
    cross = [(i, i ^ 1) for i in range(count)]
    split = SPANS[0][1]
    cut = split * 2 * HEAD_WIDTH
    marked = prepare_early(keyvalue, doc_ids, cut)
    rest, pick, mode = prepare_late(keyvalue, owner_tiles, tile_counts, cut)
    far_early, near_early = send(marked, far), send(marked, near)
    far_late, near_late = send(rest, far), send(rest, near)
    first_core = lax.axis_index("seq") % CORES == 0

    near_crossed = send(near_early, cross)
    under_crossed = send(jnp.where(first_core, marked, far_early), cross)
    early = [near_crossed, under_crossed, near_early, under_crossed, far_early, marked]
    part, out = attend(pick, queries, early, 0, early, None, *SPANS[0])
    part, far_late, near_late = lax.optimization_barrier((part, far_late, near_late))
    under = jnp.where(first_core, rest, far_late)
    crossed = send(jnp.concatenate([near_late, under], axis=0), cross)
    late = [crossed, crossed, near_late, crossed, far_late, rest]

    up = [(i, i + half) for i in range(half)]
    down = [(i + half, i) for i in range(half)]
    starts = [first * GROUP_COLS for first, _ in SPANS]

    def moving(pairs):
        def branch(pick, queries, part, out, early, late):
            got = []
            for first, last in SPANS[1:]:
                if pairs:
                    got.append(send(part, pairs))
                part, out = attend(pick, queries, late, split, early, out, first, last)
            if pairs:
                got.append(send(part, pairs))
                for part, start in zip(got, starts):
                    out = deliver(pick, [part], [start], out)
            return out

        return branch

    branches = [moving(None), moving(up), moving(down), moving(up + down)]
    return lax.switch(mode[0], branches, pick, queries, part, out, early, late)


def solution(mesh):
    placed = (
        P(("groups", "seq"), None),
        P(("groups", "seq"), None),
        P(("groups", "seq")),
        P(("groups", "seq"), None),
        P(("groups", "seq")),
    )
    return jax.shard_map(
        local, mesh=mesh, in_specs=placed, out_specs=P(("groups", "seq"), None), check_vma=False
    )
```

```python
import functools
import math

import jax
import jax.numpy as jnp
from jax import lax
from jax.experimental import pallas as pl
from jax.experimental.pallas import tpu as pltpu
from jax.sharding import PartitionSpec as P

QUERY_HEADS = 64
KEY_VALUE_HEADS = 8
HEAD_WIDTH = 128
TILE = 128
DOCUMENT_LIMIT = 512
GROUP = QUERY_HEADS // KEY_VALUE_HEADS
GROUP_COLS = GROUP * HEAD_WIDTH
MARK_ROWS = 16
NEAR_BLOCKS = 3
CORES = 2
STACK = 8
SPANS = ((0, 3), (3, 6), (6, 8))
MASKED = -1e30
IN_HBM = pl.BlockSpec(memory_space=pltpu.HBM)


def send(block, pairs):
    return lax.ppermute(block, "seq", pairs)


def stacked_rows(ref, out_ref, first):
    rows, cols = ref.shape
    for c in range(first, cols // HEAD_WIDTH):
        out_ref[(c - first) * rows : (c - first + 1) * rows, :] = ref[:, c * HEAD_WIDTH : (c + 1) * HEAD_WIDTH]


def early_kernel(doc_ref, kv_ref, early_ref):
    stacked_rows(kv_ref, early_ref, 0)
    marks = (doc_ref[...] + 1).astype(jnp.float32)
    early_ref[early_ref.shape[0] - MARK_ROWS :, :] = jnp.broadcast_to(marks, (MARK_ROWS, marks.shape[1])).astype(
        jnp.bfloat16
    )


def prepare_early(keyvalue, doc_ids, cut):
    rows = keyvalue.shape[0]
    shape = (rows * cut // HEAD_WIDTH + MARK_ROWS, HEAD_WIDTH)
    return pl.pallas_call(
        early_kernel,
        grid=(1,),
        in_specs=[pl.BlockSpec((1, rows), lambda i: (0, 0)), pl.BlockSpec((rows, cut), lambda i: (0, 0))],
        out_specs=pl.BlockSpec(shape, lambda i: (0, 0)),
        out_shape=jax.ShapeDtypeStruct(shape, jnp.bfloat16),
    )(doc_ids.reshape(1, rows), keyvalue)


def late_kernel(first, kv_ref, tiles_ref, counts_ref, late_ref, pick_ref, mode_ref):
    stacked_rows(kv_ref, late_ref, first)
    me = lax.axis_index("seq")
    held = counts_ref[0]
    for slot in range(pick_ref.shape[0]):
        kind = jnp.where(tiles_ref[0, slot] == me, 1, 2)
        pick_ref[slot] = jnp.where(slot < held, kind, 0).astype(jnp.int32)
    lower = me < lax.axis_size("seq") // 2
    alone = jnp.where((held == 0) == lower, 1, 2)
    mode_ref[0] = jnp.where(held == 1, jnp.where(tiles_ref[0, 0] == me, 0, 3), alone).astype(jnp.int32)


def prepare_late(keyvalue, owner_tiles, tile_counts, cut):
    rows, cols = keyvalue.shape
    slots = owner_tiles.shape[1]
    scalars = pl.BlockSpec(memory_space=pltpu.SMEM)
    shape = (rows * (cols - cut) // HEAD_WIDTH, HEAD_WIDTH)
    return pl.pallas_call(
        functools.partial(late_kernel, cut // HEAD_WIDTH),
        grid=(1,),
        in_specs=[pl.BlockSpec((rows, cols), lambda i: (0, 0))] + [scalars] * 2,
        out_specs=[pl.BlockSpec(shape, lambda i: (0, 0))] + [scalars] * 2,
        out_shape=[
            jax.ShapeDtypeStruct(shape, jnp.bfloat16),
            jax.ShapeDtypeStruct((slots,), jnp.int32),
            jax.ShapeDtypeStruct((1,), jnp.int32),
        ],
    )(keyvalue, owner_tiles, tile_counts)


def attend_kernel(first, span, offset, chained, pick_ref, q_hbm, *refs):
    kv_refs, mark_refs = refs[:6], refs[6:12]
    scratch = refs[12 + chained :]
    part_ref, out_ref, q_buf, kv_buf, o_buf, blank, marks, bias = scratch[:8]
    q_sems, kv_sems, o_sems, blank_sems, mark_sems = scratch[8:]
    rows = q_buf.shape[1]
    slots = pick_ref.shape[0]
    first_core = lax.axis_index("seq") % CORES == 0
    rate = HEAD_WIDTH**-0.5 * math.log2(math.e)
    mark_place = mark_refs[0].shape[0] - MARK_ROWS

    def by_distance(use, first, last):
        for b, by_core in enumerate(((5, 5), (0, 1), (2, 2), (3, 0), (4, 4))[first:last], first):
            if by_core[0] == by_core[1]:
                use(b, by_core[0])
            else:
                pl.when(first_core)(functools.partial(use, b, by_core[0]))
                pl.when(jnp.logical_not(first_core))(functools.partial(use, b, by_core[1]))

    def cols_of(g, width):
        return pl.ds(pl.multiple_of(g * width, width), width)

    def arriving_queries(g, step):
        turn = lax.rem(g, 2)
        copy = pltpu.make_async_copy(
            q_hbm.at[:, cols_of(first + g, GROUP_COLS)], q_buf.at[turn], q_sems.at[turn]
        )
        getattr(copy, step)()

    def arriving_blocks(g, step, begin, end):
        turn = lax.rem(g, 2)

        def block(b, i):
            base = kv_refs[5].shape[0] if i in (1, 3) and kv_refs[i].shape[0] > kv_refs[5].shape[0] else 0
            start = pl.multiple_of(base + (first - offset + g) * 2 * rows, MARK_ROWS)
            there = kv_refs[i].at[pl.ds(start, 2 * rows), :]
            getattr(pltpu.make_async_copy(there, kv_buf.at[turn, b], kv_sems.at[turn, b]), step)()

        by_distance(block, begin, end)

    def reading_marks(step):
        def block(b, i):
            there = mark_refs[i].at[pl.ds(mark_place, MARK_ROWS), :]
            getattr(pltpu.make_async_copy(there, marks.at[b], mark_sems.at[b]), step)()

        by_distance(block, 0, marks.shape[0])

    keeps = functools.reduce(jnp.logical_or, [pick_ref[slot] == 1 for slot in range(slots)])

    def leaving(g, step):
        turn = lax.rem(g, 2)

        @pl.when(jnp.logical_not(keeps))
        def _():
            there = part_ref.at[:, cols_of(g, GROUP_COLS)]
            getattr(pltpu.make_async_copy(o_buf.at[turn], there, o_sems.at[turn, slots]), step)()

        for slot in range(slots):
            there = out_ref.at[pl.ds(slot * rows, rows), cols_of(first + g, GROUP_COLS)]
            copy = pltpu.make_async_copy(o_buf.at[turn], there, o_sems.at[turn, slot])
            pl.when(pick_ref[slot] == 1)(getattr(copy, step))

    def clearing(step):
        for slot in range(slots):

            @pl.when(pick_ref[slot] == 0)
            def _(slot=slot):
                for g in range(span):
                    there = out_ref.at[pl.ds(slot * rows, rows), pl.ds((first + g) * GROUP_COLS, GROUP_COLS)]
                    getattr(pltpu.make_async_copy(blank, there, blank_sems.at[slot, g]), step)()

    reading_marks("start")
    arriving_queries(0, "start")
    arriving_blocks(0, "start", 0, NEAR_BLOCKS)
    blank[...] = jnp.zeros_like(blank)
    clearing("start")
    reading_marks("wait")
    third = marks[NEAR_BLOCKS, 0:1, :].astype(jnp.float32)
    reaches = jnp.max(jnp.where(third == marks[0, 0:1, 0:1].astype(jnp.float32), 1.0, 0.0)) > 0.5
    pl.when(reaches)(lambda: arriving_blocks(0, "start", NEAR_BLOCKS, marks.shape[0]))
    mine = jnp.broadcast_to(marks[0, 0:1, :].astype(jnp.float32), (rows, rows)).T
    for b in range(marks.shape[0]):
        same = mine == marks[b, 0:1, :].astype(jnp.float32)
        if b == 0:
            q_place = lax.broadcasted_iota(jnp.int32, (rows, rows), 0)
            k_place = lax.broadcasted_iota(jnp.int32, (rows, rows), 1)
            same = same & (k_place <= q_place)
        bias[:, b * rows : (b + 1) * rows] = jnp.where(same, 0.0, MASKED)

    def attention(blocks):
        held = blocks * rows

        def one_group(g, carry):
            turn = lax.rem(g, 2)

            @pl.when(g + 1 < span)
            def _():
                arriving_queries(g + 1, "start")
                arriving_blocks(g + 1, "start", 0, blocks)

            arriving_queries(g, "wait")
            arriving_blocks(g, "wait", 0, blocks)
            pl.when(g >= 2)(lambda: leaving(g - 2, "wait"))
            keys = kv_buf[turn, :blocks, :rows, :].reshape(held, HEAD_WIDTH)
            values = kv_buf[turn, :blocks, rows:, :].reshape(held, HEAD_WIDTH)
            for h in range(0, GROUP, STACK):
                q = jnp.concatenate(
                    [q_buf[turn, :, (h + i) * HEAD_WIDTH : (h + i + 1) * HEAD_WIDTH] for i in range(STACK)], axis=0
                )
                scores = lax.dot_general(q, keys, (((1,), (1,)), ((), ())), preferred_element_type=jnp.float32)
                scores = scores.reshape(STACK, rows, held) + bias[:, :held][None]
                top = jnp.max(scores, axis=2, keepdims=True)
                exponent = jnp.exp2((scores - top) * rate)
                totals = jnp.sum(exponent, axis=2, keepdims=True)
                weights = exponent.astype(jnp.bfloat16).reshape(STACK * rows, held)
                mixed = jnp.dot(weights, values, preferred_element_type=jnp.float32)
                mixed = (mixed.reshape(STACK, rows, HEAD_WIDTH) / totals).astype(jnp.bfloat16)
                for i in range(STACK):
                    o_buf[turn, :, (h + i) * HEAD_WIDTH : (h + i + 1) * HEAD_WIDTH] = mixed[i]
            leaving(g, "start")
            return carry

        lax.fori_loop(0, span, one_group, 0)

    pl.when(reaches)(lambda: attention(marks.shape[0]))
    pl.when(jnp.logical_not(reaches))(lambda: attention(NEAR_BLOCKS))
    for g in range(max(span - 2, 0), span):
        leaving(g, "wait")
    clearing("wait")


def attend(pick, queries, window, offset, marked, out, first, last):
    rows, width = queries.shape
    span = last - first
    slots = pick.shape[0]
    blocks = 5
    chained = [] if out is None else [out]
    anywhere = pl.BlockSpec(memory_space=pl.ANY)
    return pl.pallas_call(
        functools.partial(attend_kernel, first, span, offset, len(chained)),
        in_specs=[pl.BlockSpec(memory_space=pltpu.SMEM)]
        + [anywhere] * (1 + len(window) + len(marked))
        + [IN_HBM] * len(chained),
        out_specs=[anywhere, IN_HBM],
        out_shape=[
            jax.ShapeDtypeStruct((rows, span * GROUP_COLS), jnp.bfloat16),
            pltpu.HBM((slots * rows, width), jnp.bfloat16),
        ],
        input_output_aliases={2 + len(window) + len(marked): 1} if chained else {},
        scratch_shapes=[
            pltpu.VMEM((2, rows, GROUP_COLS), jnp.bfloat16),
            pltpu.VMEM((2, blocks, 2 * rows, HEAD_WIDTH), jnp.bfloat16),
            pltpu.VMEM((2, rows, GROUP_COLS), jnp.bfloat16),
            pltpu.VMEM((rows, GROUP_COLS), jnp.bfloat16),
            pltpu.VMEM((blocks, MARK_ROWS, HEAD_WIDTH), jnp.bfloat16),
            pltpu.VMEM((rows, blocks * rows), jnp.float32),
            pltpu.SemaphoreType.DMA((2,)),
            pltpu.SemaphoreType.DMA((2, blocks)),
            pltpu.SemaphoreType.DMA((2, slots + 1)),
            pltpu.SemaphoreType.DMA((slots, span)),
            pltpu.SemaphoreType.DMA((blocks,)),
        ],
        compiler_params=pltpu.CompilerParams(vmem_limit_bytes=24 * 1024 * 1024),
        cost_estimate=pl.CostEstimate(flops=0, bytes_accessed=0, transcendentals=0),
    )(pick, queries, *window, *marked, *chained)


def deliver_kernel(first_col, pieces, pick_ref, got_ref, _, out_ref, sems):
    rows, cols = got_ref.shape
    step = pl.program_id(0)

    def leaving(slot, piece):
        start = pl.multiple_of(first_col + piece * cols, cols)
        there = out_ref.at[pl.ds(slot * rows, rows), pl.ds(start, cols)]
        return pltpu.make_async_copy(got_ref, there, sems.at[piece])

    for slot in range(pick_ref.shape[0]):

        @pl.when(pick_ref[slot] == 2)
        def _(slot=slot):
            leaving(slot, step).start()

            @pl.when(step < pieces - 2)
            def _():
                leaving(slot, step).wait()

            @pl.when(step == pieces - 1)
            def _():
                for piece in range(max(pieces - 2, 0), pieces):
                    leaving(slot, piece).wait()


def deliver(pick, got, first_col, out):
    rows, cols = got.shape
    pieces = cols // GROUP_COLS
    return pl.pallas_call(
        functools.partial(deliver_kernel, first_col, pieces),
        grid=(pieces,),
        in_specs=[
            pl.BlockSpec(memory_space=pltpu.SMEM),
            pl.BlockSpec((rows, GROUP_COLS), lambda i: (0, i)),
            IN_HBM,
        ],
        out_specs=IN_HBM,
        out_shape=pltpu.HBM(out.shape, out.dtype),
        input_output_aliases={2: 0},
        scratch_shapes=[pltpu.SemaphoreType.DMA((pieces,))],
        compiler_params=pltpu.CompilerParams(vmem_limit_bytes=24 * 1024 * 1024),
    )(pick, got, out)


def local(queries, keyvalue, doc_ids, owner_tiles, tile_counts):
    count = lax.axis_size("seq")
    half = count // 2

    far = [(i, i + 2 * CORES) for i in range(count - 2 * CORES)]
    near = [(i, i + CORES) for i in range(count - CORES)]
    cross = [(i, i ^ 1) for i in range(count)]
    split = SPANS[0][1]
    cut = split * 2 * HEAD_WIDTH
    marked = prepare_early(keyvalue, doc_ids, cut)
    rest, pick, mode = prepare_late(keyvalue, owner_tiles, tile_counts, cut)
    far_early, near_early = send(marked, far), send(marked, near)
    far_late, near_late = send(rest, far), send(rest, near)
    first_core = lax.axis_index("seq") % CORES == 0

    near_crossed = send(near_early, cross)
    under_crossed = send(jnp.where(first_core, marked, far_early), cross)
    early = [near_crossed, under_crossed, near_early, under_crossed, far_early, marked]
    part, out = attend(pick, queries, early, 0, early, None, *SPANS[0])
    part, far_late, near_late = lax.optimization_barrier((part, far_late, near_late))
    under = jnp.where(first_core, rest, far_late)
    crossed = send(jnp.concatenate([near_late, under], axis=0), cross)
    late = [crossed, crossed, near_late, crossed, far_late, rest]

    up = [(i, i + half) for i in range(half)]
    down = [(i + half, i) for i in range(half)]
    starts = [first * GROUP_COLS for first, _ in SPANS]

    def moving(pairs):
        def branch(pick, queries, part, out, early, late):
            got = []
            for first, last in SPANS[1:]:
                if pairs:
                    got.append(send(part, pairs))
                part, out = attend(pick, queries, late, split, early, out, first, last)
            if pairs:
                got.append(send(part, pairs))
                for part, start in zip(got, starts):
                    out = deliver(pick, part, start, out)
            return out

        return branch

    branches = [moving(None), moving(up), moving(down), moving(up + down)]
    return lax.switch(mode[0], branches, pick, queries, part, out, early, late)


def solution(mesh):
    placed = (
        P(("groups", "seq"), None),
        P(("groups", "seq"), None),
        P(("groups", "seq")),
        P(("groups", "seq"), None),
        P(("groups", "seq")),
    )
    return jax.shard_map(
        local, mesh=mesh, in_specs=placed, out_specs=P(("groups", "seq"), None), check_vma=False
    )
```

```python
import functools
import math

import jax
import jax.numpy as jnp
from jax import lax
from jax.experimental import pallas as pl
from jax.experimental.pallas import tpu as pltpu
from jax.sharding import PartitionSpec as P

QUERY_HEADS = 64
KEY_VALUE_HEADS = 8
HEAD_WIDTH = 128
TILE = 128
DOCUMENT_LIMIT = 512
GROUP = QUERY_HEADS // KEY_VALUE_HEADS
GROUP_COLS = GROUP * HEAD_WIDTH
MARK_ROWS = 16
NEAR_BLOCKS = 3
CORES = 2
STACK = 8
SPANS = ((0, 3), (3, 6), (6, 8))
MASKED = -1e30
IN_HBM = pl.BlockSpec(memory_space=pltpu.HBM)


def send(block, pairs):
    return lax.ppermute(block, "seq", pairs)


def stacked_rows(ref, out_ref):
    rows, cols = ref.shape
    for c in range(cols // HEAD_WIDTH):
        out_ref[c * rows : (c + 1) * rows, :] = ref[:, c * HEAD_WIDTH : (c + 1) * HEAD_WIDTH]


def early_kernel(doc_ref, kv_ref, early_ref):
    stacked_rows(kv_ref, early_ref)
    marks = (doc_ref[...] + 1).astype(jnp.float32)
    early_ref[early_ref.shape[0] - MARK_ROWS :, :] = jnp.broadcast_to(marks, (MARK_ROWS, marks.shape[1])).astype(
        jnp.bfloat16
    )


def prepare_early(keyvalue, doc_ids, cut):
    rows = keyvalue.shape[0]
    shape = (rows * cut // HEAD_WIDTH + MARK_ROWS, HEAD_WIDTH)
    return pl.pallas_call(
        early_kernel,
        grid=(1,),
        in_specs=[pl.BlockSpec((1, rows), lambda i: (0, 0)), pl.BlockSpec((rows, cut), lambda i: (0, 0))],
        out_specs=pl.BlockSpec(shape, lambda i: (0, 0)),
        out_shape=jax.ShapeDtypeStruct(shape, jnp.bfloat16),
    )(doc_ids.reshape(1, rows), keyvalue)


def late_kernel(first, kv_hbm, late_ref, sems):
    rows = kv_hbm.shape[0]
    copies = []
    for c in range(late_ref.shape[0] // rows):
        columns = kv_hbm.at[:, pl.ds((first + c) * HEAD_WIDTH, HEAD_WIDTH)]
        copies.append(pltpu.make_async_copy(columns, late_ref.at[pl.ds(c * rows, rows), :], sems.at[c]))
    for copy in copies:
        copy.start()
    for copy in copies:
        copy.wait()


def prepare_late(keyvalue, cut):
    rows, cols = keyvalue.shape
    columns = (cols - cut) // HEAD_WIDTH
    shape = (rows * columns, HEAD_WIDTH)
    return pl.pallas_call(
        functools.partial(late_kernel, cut // HEAD_WIDTH),
        grid=(1,),
        in_specs=[pl.BlockSpec(memory_space=pl.ANY)],
        out_specs=pl.BlockSpec(shape, lambda i: (0, 0)),
        out_shape=jax.ShapeDtypeStruct(shape, jnp.bfloat16),
        scratch_shapes=[pltpu.SemaphoreType.DMA((columns,))],
    )(keyvalue)


def plan_kernel(tiles_ref, counts_ref, pick_ref, mode_ref):
    me = lax.axis_index("seq")
    held = counts_ref[0]
    for slot in range(pick_ref.shape[0]):
        kind = jnp.where(tiles_ref[0, slot] == me, 1, 2)
        pick_ref[slot] = jnp.where(slot < held, kind, 0).astype(jnp.int32)
    lower = me < lax.axis_size("seq") // 2
    alone = jnp.where((held == 0) == lower, 1, 2)
    mode_ref[0] = jnp.where(held == 1, jnp.where(tiles_ref[0, 0] == me, 0, 3), alone).astype(jnp.int32)


def plan(owner_tiles, tile_counts):
    scalars = pl.BlockSpec(memory_space=pltpu.SMEM)
    return pl.pallas_call(
        plan_kernel,
        in_specs=[scalars] * 2,
        out_specs=[scalars] * 2,
        out_shape=[jax.ShapeDtypeStruct((n,), jnp.int32) for n in (owner_tiles.shape[1], 1)],
    )(owner_tiles, tile_counts)


def attend_kernel(first, span, offset, chained, pick_ref, q_hbm, *refs):
    kv_refs, mark_refs = refs[:6], refs[6:12]
    scratch = refs[12 + chained :]
    part_ref, out_ref, q_buf, kv_buf, o_buf, blank, marks, bias = scratch[:8]
    q_sems, kv_sems, o_sems, blank_sems, mark_sems = scratch[8:]
    rows = q_buf.shape[1]
    slots = pick_ref.shape[0]
    first_core = lax.axis_index("seq") % CORES == 0
    rate = HEAD_WIDTH**-0.5 * math.log2(math.e)
    mark_place = mark_refs[0].shape[0] - MARK_ROWS

    def by_distance(use, first, last):
        for b, by_core in enumerate(((5, 5), (0, 1), (2, 2), (3, 0), (4, 4))[first:last], first):
            if by_core[0] == by_core[1]:
                use(b, by_core[0])
            else:
                pl.when(first_core)(functools.partial(use, b, by_core[0]))
                pl.when(jnp.logical_not(first_core))(functools.partial(use, b, by_core[1]))

    def cols_of(g, width):
        return pl.ds(pl.multiple_of(g * width, width), width)

    def arriving_queries(g, step):
        turn = lax.rem(g, 2)
        copy = pltpu.make_async_copy(
            q_hbm.at[:, cols_of(first + g, GROUP_COLS)], q_buf.at[turn], q_sems.at[turn]
        )
        getattr(copy, step)()

    def arriving_blocks(g, step, begin, end):
        turn = lax.rem(g, 2)

        def block(b, i):
            base = kv_refs[5].shape[0] if i in (1, 3) and kv_refs[i].shape[0] > kv_refs[5].shape[0] else 0
            start = pl.multiple_of(base + (first - offset + g) * 2 * rows, MARK_ROWS)
            there = kv_refs[i].at[pl.ds(start, 2 * rows), :]
            getattr(pltpu.make_async_copy(there, kv_buf.at[turn, b], kv_sems.at[turn, b]), step)()

        by_distance(block, begin, end)

    def reading_marks(step):
        def block(b, i):
            there = mark_refs[i].at[pl.ds(mark_place, MARK_ROWS), :]
            getattr(pltpu.make_async_copy(there, marks.at[b], mark_sems.at[b]), step)()

        by_distance(block, 0, marks.shape[0])

    keeps = functools.reduce(jnp.logical_or, [pick_ref[slot] == 1 for slot in range(slots)])

    def leaving(g, step):
        turn = lax.rem(g, 2)

        @pl.when(jnp.logical_not(keeps))
        def _():
            there = part_ref.at[:, cols_of(g, GROUP_COLS)]
            getattr(pltpu.make_async_copy(o_buf.at[turn], there, o_sems.at[turn, slots]), step)()

        for slot in range(slots):
            there = out_ref.at[pl.ds(slot * rows, rows), cols_of(first + g, GROUP_COLS)]
            copy = pltpu.make_async_copy(o_buf.at[turn], there, o_sems.at[turn, slot])
            pl.when(pick_ref[slot] == 1)(getattr(copy, step))

    def clearing(step):
        for slot in range(slots):

            @pl.when(pick_ref[slot] == 0)
            def _(slot=slot):
                for g in range(span):
                    there = out_ref.at[pl.ds(slot * rows, rows), pl.ds((first + g) * GROUP_COLS, GROUP_COLS)]
                    getattr(pltpu.make_async_copy(blank, there, blank_sems.at[slot, g]), step)()

    reading_marks("start")
    arriving_queries(0, "start")
    arriving_blocks(0, "start", 0, NEAR_BLOCKS)
    blank[...] = jnp.zeros_like(blank)
    clearing("start")
    reading_marks("wait")
    third = marks[NEAR_BLOCKS, 0:1, :].astype(jnp.float32)
    reaches = jnp.max(jnp.where(third == marks[0, 0:1, 0:1].astype(jnp.float32), 1.0, 0.0)) > 0.5
    pl.when(reaches)(lambda: arriving_blocks(0, "start", NEAR_BLOCKS, marks.shape[0]))
    mine = jnp.broadcast_to(marks[0, 0:1, :].astype(jnp.float32), (rows, rows)).T
    for b in range(marks.shape[0]):
        same = mine == marks[b, 0:1, :].astype(jnp.float32)
        if b == 0:
            q_place = lax.broadcasted_iota(jnp.int32, (rows, rows), 0)
            k_place = lax.broadcasted_iota(jnp.int32, (rows, rows), 1)
            same = same & (k_place <= q_place)
        bias[:, b * rows : (b + 1) * rows] = jnp.where(same, 0.0, MASKED)

    def attention(blocks):
        held = blocks * rows

        def one_group(g, carry):
            turn = lax.rem(g, 2)

            @pl.when(g + 1 < span)
            def _():
                arriving_queries(g + 1, "start")
                arriving_blocks(g + 1, "start", 0, blocks)

            arriving_queries(g, "wait")
            arriving_blocks(g, "wait", 0, blocks)
            pl.when(g >= 2)(lambda: leaving(g - 2, "wait"))
            keys = kv_buf[turn, :blocks, :rows, :].reshape(held, HEAD_WIDTH)
            values = kv_buf[turn, :blocks, rows:, :].reshape(held, HEAD_WIDTH)
            for h in range(0, GROUP, STACK):
                q = jnp.concatenate(
                    [q_buf[turn, :, (h + i) * HEAD_WIDTH : (h + i + 1) * HEAD_WIDTH] for i in range(STACK)], axis=0
                )
                scores = lax.dot_general(q, keys, (((1,), (1,)), ((), ())), preferred_element_type=jnp.float32)
                scores = scores.reshape(STACK, rows, held) + bias[:, :held][None]
                top = jnp.max(scores, axis=2, keepdims=True)
                exponent = jnp.exp2((scores - top) * rate)
                totals = jnp.sum(exponent, axis=2, keepdims=True)
                weights = exponent.astype(jnp.bfloat16).reshape(STACK * rows, held)
                mixed = jnp.dot(weights, values, preferred_element_type=jnp.float32)
                mixed = (mixed.reshape(STACK, rows, HEAD_WIDTH) / totals).astype(jnp.bfloat16)
                for i in range(STACK):
                    o_buf[turn, :, (h + i) * HEAD_WIDTH : (h + i + 1) * HEAD_WIDTH] = mixed[i]
            leaving(g, "start")
            return carry

        lax.fori_loop(0, span, one_group, 0)

    pl.when(reaches)(lambda: attention(marks.shape[0]))
    pl.when(jnp.logical_not(reaches))(lambda: attention(NEAR_BLOCKS))
    for g in range(max(span - 2, 0), span):
        leaving(g, "wait")
    clearing("wait")


def attend(pick, queries, window, offset, marked, out, first, last):
    rows, width = queries.shape
    span = last - first
    slots = pick.shape[0]
    blocks = 5
    chained = [] if out is None else [out]
    anywhere = pl.BlockSpec(memory_space=pl.ANY)
    return pl.pallas_call(
        functools.partial(attend_kernel, first, span, offset, len(chained)),
        in_specs=[pl.BlockSpec(memory_space=pltpu.SMEM)]
        + [anywhere] * (1 + len(window) + len(marked))
        + [IN_HBM] * len(chained),
        out_specs=[anywhere, IN_HBM],
        out_shape=[
            jax.ShapeDtypeStruct((rows, span * GROUP_COLS), jnp.bfloat16),
            pltpu.HBM((slots * rows, width), jnp.bfloat16),
        ],
        input_output_aliases={2 + len(window) + len(marked): 1} if chained else {},
        scratch_shapes=[
            pltpu.VMEM((2, rows, GROUP_COLS), jnp.bfloat16),
            pltpu.VMEM((2, blocks, 2 * rows, HEAD_WIDTH), jnp.bfloat16),
            pltpu.VMEM((2, rows, GROUP_COLS), jnp.bfloat16),
            pltpu.VMEM((rows, GROUP_COLS), jnp.bfloat16),
            pltpu.VMEM((blocks, MARK_ROWS, HEAD_WIDTH), jnp.bfloat16),
            pltpu.VMEM((rows, blocks * rows), jnp.float32),
            pltpu.SemaphoreType.DMA((2,)),
            pltpu.SemaphoreType.DMA((2, blocks)),
            pltpu.SemaphoreType.DMA((2, slots + 1)),
            pltpu.SemaphoreType.DMA((slots, span)),
            pltpu.SemaphoreType.DMA((blocks,)),
        ],
        compiler_params=pltpu.CompilerParams(vmem_limit_bytes=24 * 1024 * 1024),
        cost_estimate=pl.CostEstimate(flops=0, bytes_accessed=0, transcendentals=0),
    )(pick, queries, *window, *marked, *chained)


def deliver_kernel(starts, pick_ref, *refs):
    got = refs[: len(starts)]
    out_ref, sems = refs[len(starts) + 1 :]
    rows = got[0].shape[0]
    for slot in range(pick_ref.shape[0]):

        @pl.when(pick_ref[slot] == 2)
        def _(slot=slot):
            copies = [
                pltpu.make_async_copy(
                    ref, out_ref.at[pl.ds(slot * rows, rows), pl.ds(c, ref.shape[1])], sems.at[i]
                )
                for i, (ref, c) in enumerate(zip(got, starts))
            ]
            for copy in copies:
                copy.start()
            for copy in copies:
                copy.wait()


def deliver(pick, got, starts, out):
    return pl.pallas_call(
        functools.partial(deliver_kernel, starts),
        grid=(1,),
        in_specs=[pl.BlockSpec(memory_space=pltpu.SMEM)]
        + [pl.BlockSpec(g.shape, lambda i: (0, 0)) for g in got]
        + [IN_HBM],
        out_specs=IN_HBM,
        out_shape=pltpu.HBM(out.shape, out.dtype),
        input_output_aliases={1 + len(got): 0},
        scratch_shapes=[pltpu.SemaphoreType.DMA((len(got),))],
        compiler_params=pltpu.CompilerParams(vmem_limit_bytes=24 * 1024 * 1024),
    )(pick, *got, out)


def local(queries, keyvalue, doc_ids, owner_tiles, tile_counts):
    count = lax.axis_size("seq")
    half = count // 2

    far = [(i, i + 2 * CORES) for i in range(count - 2 * CORES)]
    near = [(i, i + CORES) for i in range(count - CORES)]
    cross = [(i, i ^ 1) for i in range(count)]
    split = SPANS[0][1]
    cut = split * 2 * HEAD_WIDTH
    marked = prepare_early(keyvalue, doc_ids, cut)
    rest = prepare_late(keyvalue, cut)
    pick, mode = plan(owner_tiles, tile_counts)
    far_early, near_early = send(marked, far), send(marked, near)
    far_late, near_late = send(rest, far), send(rest, near)
    first_core = lax.axis_index("seq") % CORES == 0

    near_crossed = send(near_early, cross)
    under_crossed = send(jnp.where(first_core, marked, far_early), cross)
    early = [near_crossed, under_crossed, near_early, under_crossed, far_early, marked]
    part, out = attend(pick, queries, early, 0, early, None, *SPANS[0])
    part, far_late, near_late = lax.optimization_barrier((part, far_late, near_late))
    under = jnp.where(first_core, rest, far_late)
    crossed = send(jnp.concatenate([near_late, under], axis=0), cross)
    late = [crossed, crossed, near_late, crossed, far_late, rest]

    up = [(i, i + half) for i in range(half)]
    down = [(i + half, i) for i in range(half)]
    starts = [first * GROUP_COLS for first, _ in SPANS]

    def moving(pairs):
        def branch(pick, queries, part, out, early, late):
            got = []
            for first, last in SPANS[1:]:
                if pairs:
                    got.append(send(part, pairs))
                part, out = attend(pick, queries, late, split, early, out, first, last)
            if pairs:
                got.append(send(part, pairs))
                for part, start in zip(got, starts):
                    out = deliver(pick, [part], [start], out)
            return out

        return branch

    branches = [moving(None), moving(up), moving(down), moving(up + down)]
    return lax.switch(mode[0], branches, pick, queries, part, out, early, late)


def solution(mesh):
    placed = (
        P(("groups", "seq"), None),
        P(("groups", "seq"), None),
        P(("groups", "seq")),
        P(("groups", "seq"), None),
        P(("groups", "seq")),
    )
    return jax.shard_map(
        local, mesh=mesh, in_specs=placed, out_specs=P(("groups", "seq"), None), check_vma=False
    )
```
